1024 devices in a mesh: node: 16 (over y, core), local: 64 (over z, x).
Axes of the slice: x: 8, y: 8, z: 8, core: 2. Of those that a mesh axis runs over, the one named last changes fastest.
Arguments:
- out_grad: bfloat16 [8192, 7168], P(('node', 'local')), may hold values from -6 to 6
- expert_ids: int32 [8192, 8], P(('node', 'local')), may hold values from 0 to 127, as said below
- route_weights: bfloat16 [8192, 8], P(('node', 'local')), may hold values from 0.099609375 to 0.59765625
- down_weight: bfloat16 [1024, 1024, 896], P(('node', 'local')), may hold values from -0.0625 to 0.0625
- gate_pre: bfloat16 [1024, 1024, 128], P(('node', 'local')), may hold values from -6 to 6
- up_pre: bfloat16 [1024, 1024, 128], P(('node', 'local')), may hold values from -6 to 6
Outputs:
- grad_pre: bfloat16 [1024, 2, 1024, 128], P(('node', 'local'))
- grad_weights: float32 [8192, 8], P(('node', 'local'))
The draws below stay inside these ranges and needn't reach their ends.
Inputs may be any that keep to these rules, and one draw needn't show every extreme that they name: `expert_ids`: each token names 8 different experts, two in each of four different groups (expert e belongs to group e // 8). The 8 tokens of one device reach every group exactly 2 times. Of the 32 tokens on the devices of one local index that reach one group, at most 16 name any one expert of that group, and for every group and local index some expert is named by exactly 16 of them.
All inputs are finite; a program needn't handle non-finite values.
Results may differ from the reference program's by a relative error of at most 0.013.
Values may be sent and summed in bfloat16 or wider, within the bound.
No kernel may reach another device: no remote copies, remote signals or barrier semaphores. Data moves between devices by JAX's collectives and lax.ppermute only.
A program may use at most 32 MiB of HBM per device.

```python
import jax
import jax.numpy as jnp
from jax import lax

D = 7168
HID = 1024
EPG = 8
TOPK = 8
TOK_DEV = 8
SHARDS = 8
EXPERTS = 128
DS = 896
HB = 128
SLOTS = 1024
TOKENS = 8192
N_NODE = 16
N_LOCAL = 64


def draw_expert_ids(key, part):
    key = jax.random.fold_in(key, 7)
    keys = jax.random.split(key, 6)
    tok_dev = TOK_DEV
    rows_relay = 4 * tok_dev
    cap_group = 4 * tok_dev // N_NODE
    hot_one = jax.random.randint(keys[0], (N_NODE, N_LOCAL, 1), 0, EPG)
    spread = jnp.arange(5 * tok_dev, dtype=jnp.int32) % (EPG - 1)
    even_count = jnp.sum((spread[:, None] == jnp.arange(EPG - 1, dtype=jnp.int32)[None, :]).astype(jnp.int32), axis=0)
    extra = jax.random.randint(keys[1], (N_NODE, N_LOCAL, tok_dev), 0, EPG - 1)
    extra_count = jnp.sum((extra[..., None] == jnp.arange(EPG - 1, dtype=jnp.int32)).astype(jnp.int32), axis=2)
    others = even_count + extra_count
    others = jnp.concatenate([others, jnp.zeros_like(others[..., :1])], axis=2)
    expert_iota = jnp.arange(EPG, dtype=jnp.int32)
    offset = (expert_iota[None, None, :] - hot_one - 1) % EPG
    picked = jnp.take_along_axis(others, offset, axis=2)
    counts = jnp.where(expert_iota[None, None, :] == hot_one, 2 * tok_dev, picked)
    bounds = jnp.cumsum(counts, axis=2)
    label_pos = jnp.arange(2 * rows_relay, dtype=jnp.int32)
    labels = jnp.sum((bounds[:, :, None, :] <= label_pos[:, None]).astype(jnp.int32), axis=3)
    first_half = labels[:, :, :rows_relay]
    second_half = labels[:, :, rows_relay:]
    row_scores = jax.random.randint(keys[2], (N_NODE, N_LOCAL, rows_relay), 0, 1 << 16) * rows_relay + jnp.arange(rows_relay, dtype=jnp.int32)
    row_order = jnp.argsort(row_scores, axis=2)
    first_half = jnp.take_along_axis(first_half, row_order, axis=2)
    second_half = jnp.take_along_axis(second_half, row_order, axis=2)
    group_scores = jax.random.randint(keys[3], (N_NODE, N_LOCAL, N_NODE), 0, 1 << 16) * N_NODE + jnp.arange(N_NODE, dtype=jnp.int32)
    group_perm = jnp.argsort(group_scores, axis=2)
    token_scores = jax.random.randint(keys[4], (N_NODE, N_LOCAL, tok_dev), 0, 1 << 16) * tok_dev + jnp.arange(tok_dev, dtype=jnp.int32)
    token_place = jnp.argsort(token_scores, axis=2)
    slot_number = 4 * token_place[..., None] + jnp.arange(4, dtype=jnp.int32)
    group_of = jnp.take_along_axis(group_perm, (slot_number % N_NODE).reshape(N_NODE, N_LOCAL, tok_dev * 4), axis=2).reshape(N_NODE, N_LOCAL, tok_dev, 4)
    rank_of = slot_number // N_NODE
    node_iota = jnp.arange(N_NODE, dtype=jnp.int32)[:, None, None, None]
    local_iota = jnp.arange(N_LOCAL, dtype=jnp.int32)[None, :, None, None]
    row_of = node_iota * cap_group + rank_of
    first_pick = first_half[group_of, local_iota, row_of]
    second_pick = second_half[group_of, local_iota, row_of]
    id_table = jnp.stack([group_of * EPG + first_pick, group_of * EPG + second_pick], axis=-1).reshape(N_NODE, N_LOCAL, tok_dev, TOPK)
    position_scores = jax.random.randint(keys[5], (N_NODE, N_LOCAL, tok_dev, TOPK), 0, 1 << 16) * TOPK + jnp.arange(TOPK, dtype=jnp.int32)
    position_perm = jnp.argsort(position_scores, axis=3)
    id_table = jnp.take_along_axis(id_table, position_perm, axis=3)
    return id_table.reshape(TOKENS, TOPK).astype(jnp.int32)


def levels(own_key, extent, cuts, low, top_value):
    def one(axis_at, shards_of):
        steps = jax.random.uniform(jax.random.fold_in(jax.random.fold_in(own_key, 6), axis_at), (shards_of,), jnp.float32, low / len(cuts), top_value / len(cuts))
        return jnp.repeat(jnp.exp(steps), extent[axis_at] // shards_of).reshape((-1,) + (1,) * (len(extent) - axis_at - 1))

    loudness = one(*cuts[0])
    for cut in cuts[1:]:
        loudness = loudness * one(*cut)
    return loudness


def noise(own_key, dims, scale, reach, cuts=(), held_as=jnp.bfloat16):
    drawn = jax.random.normal(own_key, dims, jnp.float32) * scale
    if len(cuts) > 0:
        drawn = levels(own_key, dims, cuts, -0.22, 0.18) * drawn
    return jnp.clip(drawn, min=-reach, max=reach).astype(held_as)


def setup_inputs(seed: int = 0) -> dict:
    key_list = jax.random.split(jax.random.key(seed), 7)
    out_grad = noise(key_list[0], (TOKENS, D), 1.0, 6.0, ((0, 1024),))
    expert_ids = draw_expert_ids(jax.random.fold_in(key_list[6], 71), 0)
    route_weights = jnp.clip(0.099609375 + 0.49804688 * jax.random.uniform(key_list[2], (TOKENS, TOPK), jnp.float32) ** levels(key_list[2], (TOKENS, TOPK), ((0, 1024),), -0.2, 0.2), 0.099609375, 0.59765625).astype(jnp.bfloat16)
    down_weight = noise(key_list[3], (EXPERTS * SHARDS, HID, DS), D ** -0.5, 0.0625, ((0, 1024),))
    gate_pre = noise(key_list[4], (EXPERTS * SHARDS, SLOTS, HB), 1.0, 6.0, ((0, 1024),))
    up_pre = noise(key_list[5], (EXPERTS * SHARDS, SLOTS, HB), 1.0, 6.0, ((0, 1024),))
    return dict(out_grad=out_grad, expert_ids=expert_ids, route_weights=route_weights, down_weight=down_weight, gate_pre=gate_pre, up_pre=up_pre)


def reference(out_grad, expert_ids, route_weights, down_weight, gate_pre, up_pre):
    tok_dev = TOK_DEV
    cap_group = 4 * tok_dev // N_NODE
    rows_relay = N_NODE * cap_group
    cap_expert = 2 * tok_dev
    id_table = expert_ids.reshape(N_NODE, N_LOCAL, tok_dev, TOPK)
    weight_table = route_weights.astype(jnp.float32).reshape(N_NODE, N_LOCAL, tok_dev, TOPK)
    token_index = jnp.arange(N_NODE * N_LOCAL * tok_dev, dtype=jnp.int32).reshape(N_NODE, N_LOCAL, tok_dev)
    group_iota = jnp.arange(N_NODE, dtype=jnp.int32)
    reaches = jnp.any((id_table // EPG)[..., None] == group_iota, axis=3).astype(jnp.int32)
    order_in = jnp.cumsum(reaches, axis=2) - reaches
    chosen = (reaches[:, :, None] == 1) & (order_in[:, :, None] == jnp.arange(cap_group, dtype=jnp.int32)[:, None, None])
    filled = jnp.sum(chosen.astype(jnp.int32), axis=3)
    row_token = jnp.sum(jnp.where(chosen, token_index[:, :, None, :, None], 0), axis=3)
    row_ids = jnp.sum(jnp.where(chosen[..., None], id_table[:, :, None, :, None, :], 0), axis=3) + filled[..., None] - 1
    row_weights = jnp.sum(jnp.where(chosen[..., None], weight_table[:, :, None, :, None, :], jnp.float32(0.0)), axis=3)
    row_token = row_token.transpose(3, 1, 0, 2).reshape(N_NODE, N_LOCAL, rows_relay)
    row_ids = row_ids.transpose(3, 1, 0, 2, 4).reshape(N_NODE, N_LOCAL, rows_relay, TOPK)
    row_weights = row_weights.transpose(3, 1, 0, 2, 4).reshape(N_NODE, N_LOCAL, rows_relay, TOPK)
    local_ids = row_ids - (group_iota * EPG)[:, None, None, None]
    member = local_ids[..., None] == jnp.arange(EPG, dtype=jnp.int32)
    named_by = jnp.any(member, axis=3).astype(jnp.int32)
    slot_of = jnp.cumsum(named_by, axis=2) - named_by
    codes_row = row_token[..., None] * TOPK + jnp.arange(TOPK, dtype=jnp.int32)
    code_each = jnp.sum(jnp.where(member, codes_row[..., None], 0), axis=3)
    weight_each = jnp.sum(jnp.where(member, row_weights[..., None], jnp.float32(0.0)), axis=3)
    assign = (named_by[:, :, None] == 1) & (slot_of[:, :, None] == jnp.arange(cap_expert, dtype=jnp.int32)[:, None, None])
    is_used = jnp.any(assign, axis=3)
    slot_code = jnp.where(is_used, jnp.sum(jnp.where(assign, code_each[:, :, None], 0), axis=3), -1)
    slot_weight = jnp.sum(jnp.where(assign, weight_each[:, :, None], jnp.float32(0.0)), axis=3)
    slot_code = slot_code.transpose(0, 3, 1, 2).reshape(EXPERTS, SLOTS)
    slot_weight = slot_weight.transpose(0, 3, 1, 2).reshape(EXPERTS, SLOTS)

    def expert_step(operands):
        codes, slot_w, weight_blocks, gate_blocks, up_blocks = operands
        is_valid = codes >= 0
        token_of = jnp.where(is_valid, codes // TOPK, 0)
        picked = jnp.where(is_valid[:, None], out_grad[token_of], jnp.zeros((), out_grad.dtype)).astype(jnp.float32)
        picked = picked.reshape(SLOTS, SHARDS, DS)
        matrix = weight_blocks.astype(jnp.float32)
        partials = jnp.einsum("qsd,shd->sqh", picked, matrix, precision=lax.Precision.HIGHEST)
        rounded = lax.optimization_barrier(partials.astype(jnp.bfloat16))
        grad_hidden = jnp.sum(rounded.astype(jnp.float32), axis=0)
        pre_gate = gate_blocks.transpose(1, 0, 2).reshape(SLOTS, HID).astype(jnp.float32)
        pre_up = up_blocks.transpose(1, 0, 2).reshape(SLOTS, HID).astype(jnp.float32)
        gating = jax.nn.sigmoid(pre_gate)
        silu_value = pre_gate * gating
        hidden_act = silu_value * pre_up
        scaled = slot_w[:, None] * grad_hidden
        d_gate = scaled * pre_up * gating * (1.0 + pre_gate * (1.0 - gating))
        d_up = scaled * silu_value
        both = jnp.stack([d_gate, d_up], axis=0).astype(jnp.bfloat16)
        both = both.reshape(2, SLOTS, SHARDS, HB).transpose(2, 0, 1, 3)
        partial_dot = jnp.sum(hidden_act * grad_hidden, axis=1)
        return both, partial_dot

    grads, dots = lax.map(expert_step, (slot_code, slot_weight,
                                        down_weight.reshape(EXPERTS, SHARDS, HID, DS),
                                        gate_pre.reshape(EXPERTS, SHARDS, SLOTS, HB),
                                        up_pre.reshape(EXPERTS, SHARDS, SLOTS, HB)))
    grad_pre = grads.reshape(EXPERTS * SHARDS, 2, SLOTS, HB)
    flat_code = slot_code.reshape(-1)
    target = jnp.where(flat_code >= 0, flat_code, TOKENS * TOPK)
    grad_weights = jnp.zeros((TOKENS * TOPK,), jnp.float32).at[target].add(dots.reshape(-1), mode="drop")
    return grad_pre, grad_weights.reshape(TOKENS, TOPK)
```

```python
import functools

import jax
import jax.numpy as jnp
from jax import lax
from jax.experimental import pallas as pl
from jax.experimental.pallas import tpu as pltpu
from jax.sharding import Mesh
from jax.sharding import PartitionSpec as P

EPG = 8
LANES = 128
F32 = jnp.float32
BF16 = jnp.bfloat16


def pick_kernel(lines_ref, rows_ref, out_ref, slot_weight_ref):
    expert = pl.program_id(0)
    experts = lines_ref.shape[0] // 2
    lines = lines_ref[...]
    line = lax.broadcasted_iota(jnp.int32, lines.shape, 0)
    slot_of = jnp.sum(jnp.where(line == expert, lines, 0.0), axis=0, keepdims=True)
    weight_of = jnp.sum(jnp.where(line == expert + experts, lines, 0.0), axis=0, keepdims=True)
    _, slots, _ = out_ref.shape
    slot = lax.broadcasted_iota(jnp.int32, (slots, lines.shape[1]), 0).astype(F32)
    holds = jnp.where(slot_of == slot, 1.0, 0.0).astype(BF16)
    out_ref[0] = jnp.dot(holds, rows_ref[...], preferred_element_type=F32).astype(BF16)
    weights = jnp.broadcast_to(weight_of, (8, lines.shape[1])).astype(BF16)
    slot_weight_ref[0] = lax.dot_general(
        weights, holds, (((1,), (1,)), ((), ())), preferred_element_type=F32
    )[:1]


def pick(lines, rows, slots):
    experts = lines.shape[0] // 2
    row_count, width = rows.shape
    return pl.pallas_call(
        pick_kernel,
        grid=(experts,),
        in_specs=[
            pl.BlockSpec(lines.shape, lambda e: (0, 0)),
            pl.BlockSpec(rows.shape, lambda e: (0, 0)),
        ],
        out_specs=[
            pl.BlockSpec((1, slots, width), lambda e: (e, 0, 0)),
            pl.BlockSpec((1, 1, slots), lambda e: (e, 0, 0)),
        ],
        out_shape=[
            jax.ShapeDtypeStruct((experts, slots, width), BF16),
            jax.ShapeDtypeStruct((experts, 1, slots), F32),
        ],
        compiler_params=pltpu.CompilerParams(vmem_limit_bytes=32 * 1024 * 1024),
        cost_estimate=pl.CostEstimate(
            flops=2 * experts * slots * row_count * width, bytes_accessed=2_500_000, transcendentals=0
        ),
    )(lines, rows)


def as_line(column):
    count = column.shape[0]
    same = lax.broadcasted_iota(jnp.int32, (count, count), 0) == lax.broadcasted_iota(
        jnp.int32, (count, count), 1
    )
    return jnp.sum(jnp.where(same, column, 0.0), axis=0, keepdims=True)


def as_column(line):
    count = line.shape[1]
    same = lax.broadcasted_iota(jnp.int32, (count, count), 0) == lax.broadcasted_iota(
        jnp.int32, (count, count), 1
    )
    return jnp.sum(jnp.where(same, line, 0.0), axis=1, keepdims=True)


def product_kernel(rows_ref, weight_ref, hidden_ref, out_ref, dot_ref):
    rows = rows_ref[0]
    blocks, slots, width = out_ref.shape
    total = jnp.zeros((slots, width), F32)
    for block in range(blocks):
        term = lax.dot_general(
            rows,
            weight_ref[0, block * width : (block + 1) * width, :],
            (((1,), (1,)), ((), ())),
            preferred_element_type=F32,
        ).astype(BF16)
        out_ref[block] = term
        total += term.astype(F32) * hidden_ref[block].astype(F32)
    dot_ref[0] = as_line(jnp.sum(total, axis=1, keepdims=True))


def product(rows, weight, hidden):
    z_count, slots, width = rows.shape
    blocks, _, lanes = hidden.shape
    units = weight.shape[1]
    return pl.pallas_call(
        product_kernel,
        grid=(z_count,),
        in_specs=[
            pl.BlockSpec((1, slots, width), lambda z: (z, 0, 0)),
            pl.BlockSpec((1, units, width), lambda z: (0, 0, 0)),
            pl.BlockSpec((blocks, slots, lanes), lambda z: (0, z, 0)),
        ],
        out_specs=[
            pl.BlockSpec((blocks, slots, lanes), lambda z: (0, z, 0)),
            pl.BlockSpec((1, 1, slots), lambda z: (z, 0, 0)),
        ],
        out_shape=[
            jax.ShapeDtypeStruct((blocks, z_count * slots, lanes), BF16),
            jax.ShapeDtypeStruct((z_count, 1, slots), F32),
        ],
        compiler_params=pltpu.CompilerParams(vmem_limit_bytes=32 * 1024 * 1024),
        cost_estimate=pl.CostEstimate(
            flops=2 * z_count * slots * width * units, bytes_accessed=8_000_000, transcendentals=0
        ),
    )(rows, weight, hidden)


def gate_kernel(u_ref, gate_ref, up_ref, weight_ref, grad_ref):
    u = u_ref[...].astype(F32)
    a = gate_ref[0].astype(F32)
    b = up_ref[0].astype(F32)
    s = 1.0 / (1.0 + jnp.exp(-a))
    scaled = as_column(weight_ref[0]) * u
    grad_ref[0, 0] = (scaled * b * s * (1.0 + a * (1.0 - s))).astype(BF16)
    grad_ref[0, 1] = (scaled * a * s).astype(BF16)


def gate(u, gate_pre, up_pre, slot_weight):
    z_count, _, slots = slot_weight.shape
    slot_count, width = u.shape
    return pl.pallas_call(
        gate_kernel,
        grid=(z_count,),
        in_specs=[
            pl.BlockSpec((slots, width), lambda z: (z, 0)),
            pl.BlockSpec((1, slots, width), lambda z: (0, z, 0)),
            pl.BlockSpec((1, slots, width), lambda z: (0, z, 0)),
            pl.BlockSpec((1, 1, slots), lambda z: (z, 0, 0)),
        ],
        out_specs=pl.BlockSpec((1, 2, slots, width), lambda z: (0, 0, z, 0)),
        out_shape=jax.ShapeDtypeStruct((1, 2, slot_count, width), BF16),
        compiler_params=pltpu.CompilerParams(vmem_limit_bytes=32 * 1024 * 1024),
        cost_estimate=pl.CostEstimate(
            flops=20 * slot_count * width, bytes_accessed=2_000_000, transcendentals=slot_count * width
        ),
    )(u, gate_pre, up_pre, slot_weight)


def body(out_grad, expert_ids, route_weights, down_weight, gate_pre, up_pre):
    n_node = lax.axis_size("node")
    n_z = lax.axis_size("z")
    n_x = lax.axis_size("x")
    tok_dev, model_width = out_grad.shape
    top_count = expert_ids.shape[1]
    width = model_width // n_x
    cap_group = 4 * tok_dev // n_node
    cap_expert = 2 * tok_dev
    slots = n_x * cap_expert
    row_count = n_node * n_x * cap_group
    tiles = width // LANES

    a = gate_pre[0].astype(F32)
    hidden = (a * (1.0 / (1.0 + jnp.exp(-a))) * up_pre[0].astype(F32)).astype(BF16)
    hidden_all = lax.all_gather(hidden, "x", tiled=True).reshape(n_x, hidden.shape[0], LANES)

    group_iota = jnp.arange(n_node, dtype=jnp.int32)
    reaches = jnp.any((expert_ids // n_z)[:, :, None] == group_iota, axis=1).astype(jnp.int32)
    order_in = jnp.cumsum(reaches, axis=0) - reaches
    chosen = (
        (reaches.T[:, None, :] == 1)
        & (order_in.T[:, None, :] == jnp.arange(cap_group, dtype=jnp.int32)[None, :, None])
    ).astype(BF16)
    named = jnp.concatenate([expert_ids.astype(BF16), route_weights], axis=1)
    source = jnp.concatenate([out_grad, jnp.pad(named, ((0, 0), (0, LANES - 2 * top_count)))], axis=1)
    send = jnp.einsum("gkt,td->gkd", chosen, source, preferred_element_type=F32).astype(BF16)
    send = send.reshape(n_node, cap_group, n_x * tiles + 1, LANES)
    data = send[:, :, : n_x * tiles].reshape(n_node, cap_group, n_x, tiles, LANES)
    tail = jnp.broadcast_to(send[:, :, None, n_x * tiles :], (n_node, cap_group, n_x, 1, LANES))
    send = jnp.concatenate([data, tail], axis=3).transpose(0, 2, 1, 3, 4)
    send = send.reshape(n_node * n_x, cap_group * (tiles + 1), LANES)
    got = lax.all_to_all(send, ("node", "x"), split_axis=0, concat_axis=0, tiled=True)
    got = got.reshape(row_count, tiles + 1, LANES)

    rows = got[:, :tiles].reshape(row_count, width)
    ids = got[:, tiles, :top_count].astype(F32).astype(jnp.int32)
    weights = got[:, tiles, top_count : 2 * top_count].astype(F32)
    my_group = lax.axis_index("node")
    member = (ids - my_group * n_z)[:, None, :] == jnp.arange(n_z, dtype=jnp.int32)[None, :, None]
    named_by = jnp.any(member, axis=2)
    weight_each = jnp.sum(jnp.where(member, weights[:, None, :], 0.0), axis=2)
    row = jnp.arange(row_count, dtype=jnp.int32)
    relay = row // cap_group % n_x
    earlier = (row[None, :] < row[:, None]) & (relay[None, :] == relay[:, None])
    place = jnp.dot(earlier.astype(BF16), named_by.astype(BF16), preferred_element_type=F32)
    slot_each = jnp.where(named_by, (relay * cap_expert).astype(F32)[:, None] + place, -1.0)
    lines = jnp.concatenate([slot_each.T, weight_each.T], axis=0)
    picked, slot_weight = pick(lines, rows, slots)
    taken = lax.all_to_all(picked, "z", split_axis=0, concat_axis=0, tiled=True)

    partial, dots = product(taken, down_weight, hidden_all)
    u = lax.psum_scatter(
        partial.reshape(n_x * n_z * slots, LANES), "x", scatter_dimension=0, tiled=True
    )

    both = jnp.concatenate([dots, slot_weight], axis=1)
    both = lax.all_to_all(both, "z", split_axis=0, concat_axis=0, tiled=True)
    dots = both[:, 0]
    grad_pre = gate(u, gate_pre, up_pre, both[:, 1:])
    slot_iota = jnp.arange(slots, dtype=jnp.int32).astype(F32)
    value = jnp.sum(
        jnp.where(slot_each[:, :, None] == slot_iota, dots[None], 0.0), axis=2
    )
    value = jnp.sum(jnp.where(member, value[:, :, None], 0.0), axis=1)
    value = value.reshape(n_node * n_x, cap_group, top_count)
    back = lax.all_to_all(value, ("node", "x"), split_axis=0, concat_axis=0, tiled=True)
    back = jnp.sum(back.reshape(n_node, n_x, cap_group, top_count), axis=1)
    grad_weights = jnp.sum(chosen.astype(F32)[..., None] * back[:, :, None, :], axis=(0, 1))
    return (grad_pre, grad_weights)


def solution(mesh):
    devices = mesh.devices
    n_node, n_local = devices.shape
    split = Mesh(devices.reshape(n_node, EPG, n_local // EPG), ("node", "z", "x"))
    first = ("node", "z", "x")
    return jax.shard_map(
        body,
        mesh=split,
        in_specs=(
            P(first, None),
            P(first, None),
            P(first, None),
            P(first, None, None),
            P(first, None, None),
            P(first, None, None),
        ),
        out_specs=(P(first, None, None, None), P(first, None)),
        check_vma=False,
    )
```

```python
import functools

import jax
import jax.numpy as jnp
from jax import lax
from jax.experimental import pallas as pl
from jax.experimental.pallas import tpu as pltpu
from jax.sharding import Mesh
from jax.sharding import PartitionSpec as P

EPG = 8
LANES = 128
F32 = jnp.float32
BF16 = jnp.bfloat16


def pick_kernel(lines_ref, rows_ref, out_ref, slot_weight_ref):
    expert = pl.program_id(0)
    experts = lines_ref.shape[0] // 2
    lines = lines_ref[...]
    line = lax.broadcasted_iota(jnp.int32, lines.shape, 0)
    slot_of = jnp.sum(jnp.where(line == expert, lines, 0.0), axis=0, keepdims=True)
    weight_of = jnp.sum(jnp.where(line == expert + experts, lines, 0.0), axis=0, keepdims=True)
    _, slots, _ = out_ref.shape
    slot = lax.broadcasted_iota(jnp.int32, (slots, lines.shape[1]), 0).astype(F32)
    holds = jnp.where(slot_of == slot, 1.0, 0.0).astype(BF16)
    out_ref[0] = jnp.dot(holds, rows_ref[...], preferred_element_type=F32).astype(BF16)
    weights = jnp.broadcast_to(weight_of, (8, lines.shape[1])).astype(BF16)
    slot_weight_ref[0] = lax.dot_general(
        weights, holds, (((1,), (1,)), ((), ())), preferred_element_type=F32
    )[:1]


def pick(lines, rows, slots):
    experts = lines.shape[0] // 2
    row_count, width = rows.shape
    return pl.pallas_call(
        pick_kernel,
        grid=(experts,),
        in_specs=[
            pl.BlockSpec(lines.shape, lambda e: (0, 0)),
            pl.BlockSpec(rows.shape, lambda e: (0, 0)),
        ],
        out_specs=[
            pl.BlockSpec((1, slots, width), lambda e: (e, 0, 0)),
            pl.BlockSpec((1, 1, slots), lambda e: (e, 0, 0)),
        ],
        out_shape=[
            jax.ShapeDtypeStruct((experts, slots, width), BF16),
            jax.ShapeDtypeStruct((experts, 1, slots), F32),
        ],
        compiler_params=pltpu.CompilerParams(vmem_limit_bytes=60 * 1024 * 1024),
        cost_estimate=pl.CostEstimate(
            flops=2 * experts * slots * row_count * width, bytes_accessed=2_500_000, transcendentals=0
        ),
    )(lines, rows)


def as_line(column):
    count = column.shape[0]
    same = lax.broadcasted_iota(jnp.int32, (count, count), 0) == lax.broadcasted_iota(
        jnp.int32, (count, count), 1
    )
    return jnp.sum(jnp.where(same, column, 0.0), axis=0, keepdims=True)


def as_column(line):
    count = line.shape[1]
    same = lax.broadcasted_iota(jnp.int32, (count, count), 0) == lax.broadcasted_iota(
        jnp.int32, (count, count), 1
    )
    return jnp.sum(jnp.where(same, line, 0.0), axis=1, keepdims=True)


def product_kernel(rows_ref, weight_ref, hidden_ref, out_ref, dot_ref, total):
    step = pl.program_id(0)
    z_count, slots, width = rows_ref.shape
    rows = rows_ref[...].reshape(z_count * slots, width)
    term = lax.dot_general(
        rows, weight_ref[0], (((1,), (1,)), ((), ())), preferred_element_type=F32
    ).astype(BF16)
    dots = jnp.where(step == 0, 0.0, total[...])
    for block in range(out_ref.shape[0]):
        part = term[:, block * LANES : (block + 1) * LANES]
        out_ref[block] = part
        dots += part.astype(F32) * hidden_ref[block].astype(F32)
    total[...] = dots

    @pl.when(step == pl.num_programs(0) - 1)
    def _():
        for z in range(z_count):
            summed = jnp.sum(total[z * slots : (z + 1) * slots, :], axis=1, keepdims=True)
            dot_ref[z] = as_line(summed)


def product(rows, weight, hidden):
    z_count, slots, width = rows.shape
    blocks, slot_count, lanes = hidden.shape
    units = weight.shape[1]
    per_step = 2
    return pl.pallas_call(
        product_kernel,
        grid=(blocks // per_step,),
        in_specs=[
            pl.BlockSpec((z_count, slots, width), lambda i: (0, 0, 0)),
            pl.BlockSpec((1, per_step * lanes, width), lambda i: (0, i, 0)),
            pl.BlockSpec((per_step, slot_count, lanes), lambda i: (i, 0, 0)),
        ],
        out_specs=[
            pl.BlockSpec((per_step, slot_count, lanes), lambda i: (i, 0, 0)),
            pl.BlockSpec((z_count, 1, slots), lambda i: (0, 0, 0)),
        ],
        out_shape=[
            jax.ShapeDtypeStruct((blocks, slot_count, lanes), BF16),
            jax.ShapeDtypeStruct((z_count, 1, slots), F32),
        ],
        scratch_shapes=[pltpu.VMEM((slot_count, lanes), F32)],
        compiler_params=pltpu.CompilerParams(vmem_limit_bytes=52 * 1024 * 1024),
        cost_estimate=pl.CostEstimate(
            flops=2 * slot_count * width * units, bytes_accessed=8_000_000, transcendentals=0
        ),
    )(rows, weight, hidden)


def gate_kernel(u_ref, gate_ref, up_ref, weight_ref, grad_ref):
    u = u_ref[...].astype(F32)
    a = gate_ref[0].astype(F32)
    b = up_ref[0].astype(F32)
    s = 1.0 / (1.0 + jnp.exp(-a))
    weight = jnp.concatenate([as_column(weight_ref[z]) for z in range(weight_ref.shape[0])], axis=0)
    scaled = weight * u
    grad_ref[0, 0] = (scaled * b * s * (1.0 + a * (1.0 - s))).astype(BF16)
    grad_ref[0, 1] = (scaled * a * s).astype(BF16)


def gate(u, gate_pre, up_pre, slot_weight):
    z_count, _, slots = slot_weight.shape
    slot_count, width = u.shape
    per_step = z_count // 2
    lines = per_step * slots
    return pl.pallas_call(
        gate_kernel,
        grid=(2,),
        in_specs=[
            pl.BlockSpec((lines, width), lambda z: (z, 0)),
            pl.BlockSpec((1, lines, width), lambda z: (0, z, 0)),
            pl.BlockSpec((1, lines, width), lambda z: (0, z, 0)),
            pl.BlockSpec((per_step, 1, slots), lambda z: (z, 0, 0)),
        ],
        out_specs=pl.BlockSpec((1, 2, lines, width), lambda z: (0, 0, z, 0)),
        out_shape=jax.ShapeDtypeStruct((1, 2, slot_count, width), BF16),
        compiler_params=pltpu.CompilerParams(vmem_limit_bytes=60 * 1024 * 1024),
        cost_estimate=pl.CostEstimate(
            flops=30 * slot_count * width, bytes_accessed=2_000_000, transcendentals=slot_count * width
        ),
    )(u, gate_pre, up_pre, slot_weight)


def body(out_grad, expert_ids, route_weights, down_weight, gate_pre, up_pre):
    n_node = lax.axis_size("node")
    n_z = lax.axis_size("z")
    n_x = lax.axis_size("x")
    tok_dev, model_width = out_grad.shape
    top_count = expert_ids.shape[1]
    width = model_width // n_x
    cap_group = 4 * tok_dev // n_node
    cap_expert = 2 * tok_dev
    slots = n_x * cap_expert
    row_count = n_node * n_x * cap_group
    tiles = width // LANES

    a = gate_pre[0].astype(F32)
    hidden = (a * (1.0 / (1.0 + jnp.exp(-a))) * up_pre[0].astype(F32)).astype(BF16)
    hidden, expert_ids, route_weights = lax.optimization_barrier((hidden, expert_ids, route_weights))
    hidden_all = lax.all_gather(hidden, "x", tiled=True).reshape(n_x, hidden.shape[0], LANES)

    group_iota = jnp.arange(n_node, dtype=jnp.int32)
    reaches = jnp.any((expert_ids // n_z)[:, :, None] == group_iota, axis=1).astype(jnp.int32)
    order_in = jnp.cumsum(reaches, axis=0) - reaches
    chosen = (
        (reaches.T[:, None, :] == 1)
        & (order_in.T[:, None, :] == jnp.arange(cap_group, dtype=jnp.int32)[None, :, None])
    ).astype(BF16)
    named = jnp.concatenate([expert_ids.astype(BF16), route_weights], axis=1)
    source = jnp.concatenate([out_grad, jnp.pad(named, ((0, 0), (0, LANES - 2 * top_count)))], axis=1)
    send = jnp.einsum("gkt,td->gkd", chosen, source, preferred_element_type=F32).astype(BF16)
    send = send.reshape(n_node, cap_group, n_x * tiles + 1, LANES)
    data = send[:, :, : n_x * tiles].reshape(n_node, cap_group, n_x, tiles, LANES)
    tail = jnp.broadcast_to(send[:, :, None, n_x * tiles :], (n_node, cap_group, n_x, 1, LANES))
    send = jnp.concatenate([data, tail], axis=3).transpose(0, 2, 1, 3, 4)
    send = send.reshape(n_node * n_x, cap_group * (tiles + 1), LANES)
    got = lax.all_to_all(send, ("node", "x"), split_axis=0, concat_axis=0, tiled=True)
    got = got.reshape(row_count, tiles + 1, LANES)

    rows = got[:, :tiles].reshape(row_count, width)
    ids = got[:, tiles, :top_count].astype(F32).astype(jnp.int32)
    weights = got[:, tiles, top_count : 2 * top_count].astype(F32)
    my_group = lax.axis_index("node")
    member = (ids - my_group * n_z)[:, None, :] == jnp.arange(n_z, dtype=jnp.int32)[None, :, None]
    named_by = jnp.any(member, axis=2)
    weight_each = jnp.sum(jnp.where(member, weights[:, None, :], 0.0), axis=2)
    row = jnp.arange(row_count, dtype=jnp.int32)
    relay = row // cap_group % n_x
    earlier = (row[None, :] < row[:, None]) & (relay[None, :] == relay[:, None])
    place = jnp.dot(earlier.astype(BF16), named_by.astype(BF16), preferred_element_type=F32)
    slot_each = jnp.where(named_by, (relay * cap_expert).astype(F32)[:, None] + place, -1.0)
    lines = jnp.concatenate([slot_each.T, weight_each.T], axis=0)
    picked, slot_weight = pick(lines, rows, slots)
    taken = lax.all_to_all(picked, "z", split_axis=0, concat_axis=0, tiled=True)

    partial, dots = product(taken, down_weight, hidden_all)
    u = lax.psum_scatter(
        partial.reshape(n_x * n_z * slots, LANES), "x", scatter_dimension=0, tiled=True
    )

    both = jnp.concatenate([dots, slot_weight], axis=1)
    both = lax.all_to_all(both, "z", split_axis=0, concat_axis=0, tiled=True)
    dots = both[:, 0]
    grad_pre = gate(u, gate_pre, up_pre, both[:, 1:])
    slot_iota = jnp.arange(slots, dtype=jnp.int32).astype(F32)
    value = jnp.sum(
        jnp.where(slot_each[:, :, None] == slot_iota, dots[None], 0.0), axis=2
    )
    value = jnp.sum(jnp.where(member, value[:, :, None], 0.0), axis=1)
    value = value.reshape(n_node * n_x, cap_group, top_count)
    back = lax.all_to_all(value, ("node", "x"), split_axis=0, concat_axis=0, tiled=True)
    back = jnp.sum(back.reshape(n_node, n_x, cap_group, top_count), axis=1)
    grad_weights = jnp.sum(chosen.astype(F32)[..., None] * back[:, :, None, :], axis=(0, 1))
    return (grad_pre, grad_weights)


def solution(mesh):
    devices = mesh.devices
    n_node, n_local = devices.shape
    split = Mesh(devices.reshape(n_node, EPG, n_local // EPG), ("node", "z", "x"))
    first = ("node", "z", "x")
    return jax.shard_map(
        body,
        mesh=split,
        in_specs=(
            P(first, None),
            P(first, None),
            P(first, None),
            P(first, None, None),
            P(first, None, None),
            P(first, None, None),
        ),
        out_specs=(P(first, None, None, None), P(first, None)),
        check_vma=False,
    )
```

```python
import functools

import jax
import jax.numpy as jnp
from jax import lax
from jax.experimental import pallas as pl
from jax.experimental.pallas import tpu as pltpu
from jax.sharding import Mesh
from jax.sharding import PartitionSpec as P

EPG = 8
LANES = 128
F32 = jnp.float32
BF16 = jnp.bfloat16


def pick_kernel(lines_ref, rows_ref, out_ref, slot_weight_ref):
    experts, slots, _ = out_ref.shape
    row_count = rows_ref.shape[0]
    slot = lax.broadcasted_iota(jnp.int32, (slots, row_count), 0).astype(F32)
    for expert in range(experts):
        holds = jnp.where(lines_ref[expert : expert + 1, :] == slot, 1.0, 0.0).astype(BF16)
        out_ref[expert] = jnp.dot(holds, rows_ref[...], preferred_element_type=F32).astype(BF16)
        weights = lines_ref[experts + expert : experts + expert + 1, :].astype(BF16)
        slot_weight_ref[expert] = lax.dot_general(
            jnp.broadcast_to(weights, (8, row_count)),
            holds,
            (((1,), (1,)), ((), ())),
            preferred_element_type=F32,
        )[:1]


def pick(lines, rows, slots):
    experts = lines.shape[0] // 2
    row_count, width = rows.shape
    vmem = pl.BlockSpec(memory_space=pltpu.VMEM)
    return pl.pallas_call(
        pick_kernel,
        in_specs=[vmem, vmem],
        out_specs=[vmem, vmem],
        out_shape=[
            jax.ShapeDtypeStruct((experts, slots, width), BF16),
            jax.ShapeDtypeStruct((experts, 1, slots), F32),
        ],
        compiler_params=pltpu.CompilerParams(vmem_limit_bytes=32 * 1024 * 1024),
        cost_estimate=pl.CostEstimate(
            flops=2 * experts * slots * row_count * width, bytes_accessed=2_500_000, transcendentals=0
        ),
    )(lines, rows)


def as_line(column):
    count = column.shape[0]
    same = lax.broadcasted_iota(jnp.int32, (count, count), 0) == lax.broadcasted_iota(
        jnp.int32, (count, count), 1
    )
    return jnp.sum(jnp.where(same, column, 0.0), axis=0, keepdims=True)


def as_column(line):
    count = line.shape[1]
    same = lax.broadcasted_iota(jnp.int32, (count, count), 0) == lax.broadcasted_iota(
        jnp.int32, (count, count), 1
    )
    return jnp.sum(jnp.where(same, line, 0.0), axis=1, keepdims=True)


def product_kernel(rows_ref, weight_ref, out_ref):
    z_count, slots, width = rows_ref.shape
    rows = rows_ref[...].reshape(z_count * slots, width)
    term = lax.dot_general(
        rows, weight_ref[0], (((1,), (1,)), ((), ())), preferred_element_type=F32
    ).astype(BF16)
    for block in range(out_ref.shape[0]):
        out_ref[block] = term[:, block * LANES : (block + 1) * LANES]


def product(rows, weight):
    z_count, slots, width = rows.shape
    units = weight.shape[1]
    slot_count = z_count * slots
    per_step = 2
    return pl.pallas_call(
        product_kernel,
        grid=(units // LANES // per_step,),
        in_specs=[
            pl.BlockSpec((z_count, slots, width), lambda i: (0, 0, 0)),
            pl.BlockSpec((1, per_step * LANES, width), lambda i: (0, i, 0)),
        ],
        out_specs=pl.BlockSpec((per_step, slot_count, LANES), lambda i: (i, 0, 0)),
        out_shape=jax.ShapeDtypeStruct((units // LANES, slot_count, LANES), BF16),
        compiler_params=pltpu.CompilerParams(vmem_limit_bytes=52 * 1024 * 1024),
        cost_estimate=pl.CostEstimate(
            flops=2 * slot_count * width * units, bytes_accessed=6_000_000, transcendentals=0
        ),
    )(rows, weight)


def dots_kernel(term_ref, hidden_ref, dot_ref):
    z_count, _, slots = dot_ref.shape
    total = term_ref[0].astype(F32) * hidden_ref[0].astype(F32)
    for block in range(1, term_ref.shape[0]):
        total += term_ref[block].astype(F32) * hidden_ref[block].astype(F32)
    for z in range(z_count):
        dot_ref[z] = as_line(jnp.sum(total[z * slots : (z + 1) * slots, :], axis=1, keepdims=True))


def dots_of(term, hidden, z_count):
    blocks, slot_count, lanes = hidden.shape
    slots = slot_count // z_count
    per_step = z_count // 4
    block = pl.BlockSpec((blocks, per_step * slots, lanes), lambda i: (0, i, 0))
    return pl.pallas_call(
        dots_kernel,
        grid=(4,),
        in_specs=[block, block],
        out_specs=pl.BlockSpec((per_step, 1, slots), lambda i: (i, 0, 0)),
        out_shape=jax.ShapeDtypeStruct((z_count, 1, slots), F32),
        compiler_params=pltpu.CompilerParams(vmem_limit_bytes=60 * 1024 * 1024),
        cost_estimate=pl.CostEstimate(
            flops=2 * blocks * slot_count * lanes, bytes_accessed=4_000_000, transcendentals=0
        ),
    )(term, hidden)


def gate_kernel(u_ref, gate_ref, up_ref, weight_ref, grad_ref):
    u = u_ref[...].astype(F32)
    a = gate_ref[0].astype(F32)
    b = up_ref[0].astype(F32)
    s = 1.0 / (1.0 + jnp.exp(-a))
    weight = jnp.concatenate([as_column(weight_ref[z]) for z in range(weight_ref.shape[0])], axis=0)
    scaled = weight * u
    grad_ref[0, 0] = (scaled * b * s * (1.0 + a * (1.0 - s))).astype(BF16)
    grad_ref[0, 1] = (scaled * a * s).astype(BF16)


def gate(u, gate_pre, up_pre, slot_weight):
    z_count, _, slots = slot_weight.shape
    slot_count, width = u.shape
    per_step = z_count // 2
    lines = per_step * slots
    return pl.pallas_call(
        gate_kernel,
        grid=(2,),
        in_specs=[
            pl.BlockSpec((lines, width), lambda z: (z, 0)),
            pl.BlockSpec((1, lines, width), lambda z: (0, z, 0)),
            pl.BlockSpec((1, lines, width), lambda z: (0, z, 0)),
            pl.BlockSpec((per_step, 1, slots), lambda z: (z, 0, 0)),
        ],
        out_specs=pl.BlockSpec((1, 2, lines, width), lambda z: (0, 0, z, 0)),
        out_shape=jax.ShapeDtypeStruct((1, 2, slot_count, width), BF16),
        compiler_params=pltpu.CompilerParams(vmem_limit_bytes=60 * 1024 * 1024),
        cost_estimate=pl.CostEstimate(
            flops=30 * slot_count * width, bytes_accessed=2_000_000, transcendentals=slot_count * width
        ),
    )(u, gate_pre, up_pre, slot_weight)


def body(out_grad, expert_ids, route_weights, down_weight, gate_pre, up_pre):
    n_node = lax.axis_size("node")
    n_z = lax.axis_size("z")
    n_x = lax.axis_size("x")
    tok_dev, model_width = out_grad.shape
    top_count = expert_ids.shape[1]
    width = model_width // n_x
    cap_group = 4 * tok_dev // n_node
    cap_expert = 2 * tok_dev
    slots = n_x * cap_expert
    row_count = n_node * n_x * cap_group
    tiles = width // LANES

    a = gate_pre[0].astype(F32)
    hidden = (a * (1.0 / (1.0 + jnp.exp(-a))) * up_pre[0].astype(F32)).astype(BF16)
    hidden_all = lax.all_gather(hidden, "x", tiled=True).reshape(n_x, hidden.shape[0], LANES)

    group_iota = jnp.arange(n_node, dtype=jnp.int32)
    reaches = jnp.any((expert_ids // n_z)[:, :, None] == group_iota, axis=1).astype(jnp.int32)
    order_in = jnp.cumsum(reaches, axis=0) - reaches
    chosen = (
        (reaches.T[:, None, :] == 1)
        & (order_in.T[:, None, :] == jnp.arange(cap_group, dtype=jnp.int32)[None, :, None])
    ).astype(BF16)
    named = jnp.concatenate([expert_ids.astype(BF16), route_weights], axis=1)
    source = jnp.concatenate([out_grad, jnp.pad(named, ((0, 0), (0, LANES - 2 * top_count)))], axis=1)
    send = jnp.einsum("gkt,td->gkd", chosen, source, preferred_element_type=F32).astype(BF16)
    send = send.reshape(n_node, cap_group, n_x * tiles + 1, LANES)
    data = send[:, :, : n_x * tiles].reshape(n_node, cap_group, n_x, tiles, LANES)
    tail = jnp.broadcast_to(send[:, :, None, n_x * tiles :], (n_node, cap_group, n_x, 1, LANES))
    send = jnp.concatenate([data, tail], axis=3).transpose(0, 2, 1, 3, 4)
    send = send.reshape(n_node * n_x, cap_group * (tiles + 1), LANES)
    got = lax.all_to_all(send, ("node", "x"), split_axis=0, concat_axis=0, tiled=True)
    got = got.reshape(row_count, tiles + 1, LANES)

    rows = got[:, :tiles].reshape(row_count, width)
    ids = got[:, tiles, :top_count].astype(F32).astype(jnp.int32)
    weights = got[:, tiles, top_count : 2 * top_count].astype(F32)
    my_group = lax.axis_index("node")
    member = (ids - my_group * n_z)[:, None, :] == jnp.arange(n_z, dtype=jnp.int32)[None, :, None]
    named_by = jnp.any(member, axis=2)
    weight_each = jnp.sum(jnp.where(member, weights[:, None, :], 0.0), axis=2)
    row = jnp.arange(row_count, dtype=jnp.int32)
    relay = row // cap_group % n_x
    earlier = (row[None, :] < row[:, None]) & (relay[None, :] == relay[:, None])
    place = jnp.dot(earlier.astype(BF16), named_by.astype(BF16), preferred_element_type=F32)
    slot_each = jnp.where(named_by, (relay * cap_expert).astype(F32)[:, None] + place, -1.0)
    lines = jnp.concatenate([slot_each.T, weight_each.T], axis=0)
    picked, slot_weight = pick(lines, rows, slots)
    taken = lax.all_to_all(picked, "z", split_axis=0, concat_axis=0, tiled=True)

    partial = product(taken, down_weight)
    dots = dots_of(partial, hidden_all, n_z)
    u = lax.psum_scatter(
        partial.reshape(n_x * n_z * slots, LANES), "x", scatter_dimension=0, tiled=True
    )

    both = jnp.concatenate([dots, slot_weight], axis=1)
    both = lax.all_to_all(both, "z", split_axis=0, concat_axis=0, tiled=True)
    dots = both[:, 0]
    grad_pre = gate(u, gate_pre, up_pre, both[:, 1:])
    slot_iota = jnp.arange(slots, dtype=jnp.int32).astype(F32)
    value = jnp.sum(
        jnp.where(slot_each[:, :, None] == slot_iota, dots[None], 0.0), axis=2
    )
    value = jnp.sum(jnp.where(member, value[:, :, None], 0.0), axis=1)
    value = value.reshape(n_node * n_x, cap_group, top_count)
    back = lax.all_to_all(value, ("node", "x"), split_axis=0, concat_axis=0, tiled=True)
    back = jnp.sum(back.reshape(n_node, n_x, cap_group, top_count), axis=1)
    grad_weights = jnp.sum(chosen.astype(F32)[..., None] * back[:, :, None, :], axis=(0, 1))
    return (grad_pre, grad_weights)


def solution(mesh):
    devices = mesh.devices
    n_node, n_local = devices.shape
    split = Mesh(devices.reshape(n_node, EPG, n_local // EPG), ("node", "z", "x"))
    first = ("node", "z", "x")
    return jax.shard_map(
        body,
        mesh=split,
        in_specs=(
            P(first, None),
            P(first, None),
            P(first, None),
            P(first, None, None),
            P(first, None, None),
            P(first, None, None),
        ),
        out_specs=(P(first, None, None, None), P(first, None)),
        check_vma=False,
    )
```

```python
import functools

import jax
import jax.numpy as jnp
from jax import lax
from jax.experimental import pallas as pl
from jax.experimental.pallas import tpu as pltpu
from jax.sharding import Mesh
from jax.sharding import PartitionSpec as P

EPG = 8
LANES = 128
F32 = jnp.float32
BF16 = jnp.bfloat16


def iota(shape, axis):
    return lax.broadcasted_iota(jnp.int32, shape, axis)


def one_where(mask):
    return jnp.where(mask, 1.0, 0.0)


def send_kernel(grad_ref, ids_ref, weights_ref, out_ref, chosen_ref, *, experts):
    nodes, slices, lines, _ = out_ref.shape
    tokens, top_count = ids_ref.shape
    tiles = grad_ref.shape[1] // slices // LANES
    parts = tiles + 1
    per_group = lines // parts
    ids = ids_ref[...].astype(F32)
    columns = parts * tokens
    spread = one_where(iota((tokens, columns), 0) == iota((tokens, columns), 1) % tokens)
    named = lax.dot_general(ids, spread, (((0,), (0,)), ((), ())), preferred_element_type=F32)
    named_group = named.astype(jnp.int32) // experts
    shape = (nodes * lines, columns)
    line, column = iota(shape, 0), iota(shape, 1)
    group, rank, part = line // lines, line // parts % per_group, line % parts
    reaches = jnp.zeros(shape, F32)
    for place in range(top_count):
        reaches = jnp.where(named_group[place : place + 1, :] == group, 1.0, reaches)
    square = (columns, columns)
    before = one_where((iota(square, 0) < tokens) & (iota(square, 0) < iota(square, 1) % tokens))
    order = jnp.dot(reaches, before, preferred_element_type=F32)
    chosen = jnp.where(
        (order == rank.astype(F32)) & (part == column // tokens), reaches, 0.0
    ).astype(BF16)
    picks = (chosen_ref.shape[0], nodes * lines)
    first_lines = one_where(iota(picks, 0) * parts == iota(picks, 1)).astype(BF16)
    chosen_ref[...] = jnp.dot(first_lines, chosen, preferred_element_type=F32)[:, :tokens]
    place = (top_count, LANES)
    tail = jnp.dot(ids, one_where(iota(place, 0) == iota(place, 1)), preferred_element_type=F32)
    tail += jnp.dot(
        weights_ref[...].astype(F32),
        one_where(iota(place, 0) + top_count == iota(place, 1)),
        preferred_element_type=F32,
    )
    for piece in range(slices):
        first = piece * tiles
        source = [
            grad_ref[:, (first + tile) * LANES : (first + tile + 1) * LANES].astype(F32) for tile in range(tiles)
        ]
        source = jnp.concatenate(source + [tail], axis=0).astype(BF16)
        rows = jnp.dot(chosen, source, preferred_element_type=F32).astype(BF16)
        out_ref[:, piece] = rows.reshape(nodes, lines, LANES)


def send_rows(out_grad, expert_ids, route_weights, nodes, slices, experts, per_group):
    lines = per_group * (out_grad.shape[1] // slices // LANES + 1)
    return pl.pallas_call(
        functools.partial(send_kernel, experts=experts),
        out_shape=[
            jax.ShapeDtypeStruct((nodes, slices, lines, LANES), BF16),
            jax.ShapeDtypeStruct((nodes * per_group, out_grad.shape[0]), F32),
        ],
        compiler_params=pltpu.CompilerParams(vmem_limit_bytes=32 * 1024 * 1024),
        cost_estimate=pl.CostEstimate(flops=40_000_000, bytes_accessed=700_000, transcendentals=0),
    )(out_grad, expert_ids, route_weights)


def pick_kernel(lines_ref, rows_ref, first_ref, second_ref, slot_weight_ref):
    experts, half, _ = first_ref.shape
    slots = 2 * half
    row_count = rows_ref.shape[0]
    slot = lax.broadcasted_iota(jnp.int32, (slots, row_count), 0).astype(F32)
    for expert in range(experts):
        holds = jnp.where(lines_ref[expert : expert + 1, :] == slot, 1.0, 0.0).astype(BF16)
        first_ref[expert] = jnp.dot(
            holds[:half], rows_ref[...], preferred_element_type=F32
        ).astype(BF16)
        second_ref[expert] = jnp.dot(
            holds[half:], rows_ref[...], preferred_element_type=F32
        ).astype(BF16)
        weights = lines_ref[experts + expert : experts + expert + 1, :].astype(BF16)
        slot_weight_ref[expert] = lax.dot_general(
            jnp.broadcast_to(weights, (8, row_count)),
            holds,
            (((1,), (1,)), ((), ())),
            preferred_element_type=F32,
        )[:1]


def pick(lines, rows, slots):
    experts = lines.shape[0] // 2
    row_count, width = rows.shape
    vmem = pl.BlockSpec(memory_space=pltpu.VMEM)
    return pl.pallas_call(
        pick_kernel,
        in_specs=[vmem, vmem],
        out_specs=[vmem, vmem, vmem],
        out_shape=[
            jax.ShapeDtypeStruct((experts, slots // 2, width), BF16),
            jax.ShapeDtypeStruct((experts, slots // 2, width), BF16),
            jax.ShapeDtypeStruct((experts, 1, slots), F32),
        ],
        compiler_params=pltpu.CompilerParams(vmem_limit_bytes=32 * 1024 * 1024),
        cost_estimate=pl.CostEstimate(
            flops=2 * experts * slots * row_count * width, bytes_accessed=2_500_000, transcendentals=0
        ),
    )(lines, rows)


def as_line(column):
    count = column.shape[0]
    same = lax.broadcasted_iota(jnp.int32, (count, count), 0) == lax.broadcasted_iota(
        jnp.int32, (count, count), 1
    )
    return jnp.sum(jnp.where(same, column, 0.0), axis=0, keepdims=True)


def as_column(line):
    count = line.shape[1]
    same = lax.broadcasted_iota(jnp.int32, (count, count), 0) == lax.broadcasted_iota(
        jnp.int32, (count, count), 1
    )
    return jnp.sum(jnp.where(same, line, 0.0), axis=1, keepdims=True)


def product_kernel(first_ref, second_ref, weight_ref, out_ref):
    z_count, half, width = first_ref.shape
    for part, rows_ref in enumerate((first_ref, second_ref)):
        rows = rows_ref[...].reshape(z_count * half, width)
        term = lax.dot_general(
            rows, weight_ref[0], (((1,), (1,)), ((), ())), preferred_element_type=F32
        ).astype(BF16)
        for block in range(out_ref.shape[0]):
            lanes = term[:, block * LANES : (block + 1) * LANES]
            out_ref[block, :, part] = lanes.reshape(z_count, half, LANES)


def product(first, second, weight):
    z_count, half, width = first.shape
    units = weight.shape[1]
    per_step = 2
    rows = pl.BlockSpec((z_count, half, width), lambda i: (0, 0, 0))
    return pl.pallas_call(
        product_kernel,
        grid=(units // LANES // per_step,),
        in_specs=[rows, rows, pl.BlockSpec((1, per_step * LANES, width), lambda i: (0, i, 0))],
        out_specs=pl.BlockSpec((per_step, z_count, 2, half, LANES), lambda i: (i, 0, 0, 0, 0)),
        out_shape=jax.ShapeDtypeStruct((units // LANES, z_count, 2, half, LANES), BF16),
        compiler_params=pltpu.CompilerParams(vmem_limit_bytes=52 * 1024 * 1024),
        cost_estimate=pl.CostEstimate(
            flops=4 * z_count * half * width * units, bytes_accessed=6_000_000, transcendentals=0
        ),
    )(first, second, weight)


def dots_kernel(term_ref, hidden_ref, weight_ref, both_ref):
    z_count, _, slots = both_ref.shape
    total = term_ref[0].astype(F32) * hidden_ref[0].astype(F32)
    for block in range(1, term_ref.shape[0]):
        total += term_ref[block].astype(F32) * hidden_ref[block].astype(F32)
    for z in range(z_count):
        both_ref[z, 0:1] = as_line(jnp.sum(total[z * slots : (z + 1) * slots, :], axis=1, keepdims=True))
        both_ref[z, 1:2] = weight_ref[z]


def dots_of(term, hidden, slot_weight):
    blocks, slot_count, lanes = hidden.shape
    z_count, _, slots = slot_weight.shape
    per_step = z_count // 4
    block = pl.BlockSpec((blocks, per_step * slots, lanes), lambda i: (0, i, 0))
    return pl.pallas_call(
        dots_kernel,
        grid=(4,),
        in_specs=[block, block, pl.BlockSpec((per_step, 1, slots), lambda i: (i, 0, 0))],
        out_specs=pl.BlockSpec((per_step, 2, slots), lambda i: (i, 0, 0)),
        out_shape=jax.ShapeDtypeStruct((z_count, 2, slots), F32),
        compiler_params=pltpu.CompilerParams(vmem_limit_bytes=60 * 1024 * 1024),
        cost_estimate=pl.CostEstimate(
            flops=2 * blocks * slot_count * lanes, bytes_accessed=4_000_000, transcendentals=0
        ),
    )(term, hidden, slot_weight)


def gate_kernel(u_ref, gate_ref, up_ref, weight_ref, grad_ref):
    u = u_ref[...].astype(F32)
    a = gate_ref[0].astype(F32)
    b = up_ref[0].astype(F32)
    s = 1.0 / (1.0 + jnp.exp(-a))
    weight = jnp.concatenate([as_column(weight_ref[z, 1:2]) for z in range(weight_ref.shape[0])], axis=0)
    scaled = weight * u
    grad_ref[0, 0] = (scaled * b * s * (1.0 + a * (1.0 - s))).astype(BF16)
    grad_ref[0, 1] = (scaled * a * s).astype(BF16)


def gate(u, gate_pre, up_pre, both):
    z_count, _, slots = both.shape
    slot_count, width = u.shape
    per_step = z_count // 2
    lines = per_step * slots
    return pl.pallas_call(
        gate_kernel,
        grid=(2,),
        in_specs=[
            pl.BlockSpec((lines, width), lambda z: (z, 0)),
            pl.BlockSpec((1, lines, width), lambda z: (0, z, 0)),
            pl.BlockSpec((1, lines, width), lambda z: (0, z, 0)),
            pl.BlockSpec((per_step, 2, slots), lambda z: (z, 0, 0)),
        ],
        out_specs=pl.BlockSpec((1, 2, lines, width), lambda z: (0, 0, z, 0)),
        out_shape=jax.ShapeDtypeStruct((1, 2, slot_count, width), BF16),
        compiler_params=pltpu.CompilerParams(vmem_limit_bytes=60 * 1024 * 1024),
        cost_estimate=pl.CostEstimate(
            flops=30 * slot_count * width, bytes_accessed=2_000_000, transcendentals=slot_count * width
        ),
    )(u, gate_pre, up_pre, both)


def body(out_grad, expert_ids, route_weights, down_weight, gate_pre, up_pre):
    n_node = lax.axis_size("node")
    n_z = lax.axis_size("z")
    n_x = lax.axis_size("x")
    tok_dev, model_width = out_grad.shape
    top_count = expert_ids.shape[1]
    width = model_width // n_x
    cap_group = 4 * tok_dev // n_node
    cap_expert = 2 * tok_dev
    slots = n_x * cap_expert
    row_count = n_node * n_x * cap_group
    tiles = width // LANES

    a = gate_pre[0].astype(F32)
    hidden = (a * (1.0 / (1.0 + jnp.exp(-a))) * up_pre[0].astype(F32)).astype(BF16)
    hidden_all = lax.all_gather(hidden, "x", tiled=True).reshape(n_x, hidden.shape[0], LANES)

    send, chosen = send_rows(out_grad, expert_ids, route_weights, n_node, n_x, n_z, cap_group)
    send = send.reshape(n_node * n_x, cap_group * (tiles + 1), LANES)
    got = lax.all_to_all(send, ("node", "x"), split_axis=0, concat_axis=0, tiled=True)
    got = got.reshape(row_count, tiles + 1, LANES)

    rows = got[:, :tiles].reshape(row_count, width)
    ids = got[:, tiles, :top_count].astype(F32).astype(jnp.int32)
    weights = got[:, tiles, top_count : 2 * top_count].astype(F32)
    my_group = lax.axis_index("node")
    member = (ids - my_group * n_z)[:, None, :] == jnp.arange(n_z, dtype=jnp.int32)[None, :, None]
    named_by = jnp.any(member, axis=2)
    weight_each = jnp.sum(jnp.where(member, weights[:, None, :], 0.0), axis=2)
    row = jnp.arange(row_count, dtype=jnp.int32)
    relay = row // cap_group % n_x
    earlier = (row[None, :] < row[:, None]) & (relay[None, :] == relay[:, None])
    place = jnp.dot(earlier.astype(BF16), named_by.astype(BF16), preferred_element_type=F32)
    slot_each = jnp.where(named_by, (relay * cap_expert).astype(F32)[:, None] + place, -1.0)
    lines = jnp.concatenate([slot_each.T, weight_each.T], axis=0)
    first, second, slot_weight = pick(lines, rows, slots)
    first = lax.all_to_all(first, "z", split_axis=0, concat_axis=0, tiled=True)
    second = lax.all_to_all(second, "z", split_axis=0, concat_axis=0, tiled=True)

    partial = product(first, second, down_weight).reshape(n_x, n_z * slots, LANES)
    u = lax.psum_scatter(
        partial.reshape(n_x * n_z * slots, LANES), "x", scatter_dimension=0, tiled=True
    )

    both = dots_of(partial, hidden_all, slot_weight)
    both = lax.all_to_all(both, "z", split_axis=0, concat_axis=0, tiled=True)
    dots = both[:, 0]
    grad_pre = gate(u, gate_pre, up_pre, both)
    slot_iota = jnp.arange(slots, dtype=jnp.int32).astype(F32)
    value = jnp.sum(
        jnp.where(slot_each[:, :, None] == slot_iota, dots[None], 0.0), axis=2
    )
    value = jnp.sum(jnp.where(member, value[:, :, None], 0.0), axis=1)
    value = value.reshape(n_node * n_x, cap_group, top_count)
    back = lax.all_to_all(value, ("node", "x"), split_axis=0, concat_axis=0, tiled=True)
    back = jnp.sum(back.reshape(n_node, n_x, cap_group, top_count), axis=1)
    chosen = chosen.reshape(n_node, cap_group, tok_dev)
    grad_weights = jnp.sum(chosen[..., None] * back[:, :, None, :], axis=(0, 1))
    return (grad_pre, grad_weights)


def solution(mesh):
    devices = mesh.devices
    n_node, n_local = devices.shape
    split = Mesh(devices.reshape(n_node, EPG, n_local // EPG), ("node", "z", "x"))
    first = ("node", "z", "x")
    return jax.shard_map(
        body,
        mesh=split,
        in_specs=(
            P(first, None),
            P(first, None),
            P(first, None),
            P(first, None, None),
            P(first, None, None),
            P(first, None, None),
        ),
        out_specs=(P(first, None, None, None), P(first, None)),
        check_vma=False,
    )
```

```python
import functools

import jax
import jax.numpy as jnp
from jax import lax
from jax.experimental import pallas as pl
from jax.experimental.pallas import tpu as pltpu
from jax.sharding import Mesh
from jax.sharding import PartitionSpec as P

EPG = 8
LANES = 128
F32 = jnp.float32
BF16 = jnp.bfloat16


def iota(shape, axis):
    return lax.broadcasted_iota(jnp.int32, shape, axis)


def one_where(mask):
    return jnp.where(mask, 1.0, 0.0)


def send_kernel(grad_ref, ids_ref, weights_ref, out_ref, chosen_ref, *, experts):
    nodes, slices, lines, _ = out_ref.shape
    tokens, top_count = ids_ref.shape
    tiles = grad_ref.shape[1] // slices // LANES
    parts = tiles + 1
    per_group = lines // parts
    ids = ids_ref[...].astype(F32)
    columns = parts * tokens
    spread = one_where(iota((tokens, columns), 0) == iota((tokens, columns), 1) % tokens)
    named = lax.dot_general(ids, spread, (((0,), (0,)), ((), ())), preferred_element_type=F32)
    named_group = named.astype(jnp.int32) // experts
    shape = (nodes * lines, columns)
    line, column = iota(shape, 0), iota(shape, 1)
    group, rank, part = line // lines, line // parts % per_group, line % parts
    reaches = jnp.zeros(shape, F32)
    for place in range(top_count):
        reaches = jnp.where(named_group[place : place + 1, :] == group, 1.0, reaches)
    square = (columns, columns)
    before = one_where((iota(square, 0) < tokens) & (iota(square, 0) < iota(square, 1) % tokens))
    order = jnp.dot(reaches, before, preferred_element_type=F32)
    chosen = jnp.where(
        (order == rank.astype(F32)) & (part == column // tokens), reaches, 0.0
    ).astype(BF16)
    picks = (chosen_ref.shape[0], nodes * lines)
    first_lines = one_where(iota(picks, 0) * parts == iota(picks, 1)).astype(BF16)
    chosen_ref[...] = jnp.dot(first_lines, chosen, preferred_element_type=F32)[:, :tokens]
    place = (top_count, LANES)
    tail = jnp.dot(ids, one_where(iota(place, 0) == iota(place, 1)), preferred_element_type=F32)
    tail += jnp.dot(
        weights_ref[...].astype(F32),
        one_where(iota(place, 0) + top_count == iota(place, 1)),
        preferred_element_type=F32,
    )
    for piece in range(slices):
        first = piece * tiles
        source = [
            grad_ref[:, (first + tile) * LANES : (first + tile + 1) * LANES].astype(F32) for tile in range(tiles)
        ]
        source = jnp.concatenate(source + [tail], axis=0).astype(BF16)
        rows = jnp.dot(chosen, source, preferred_element_type=F32).astype(BF16)
        out_ref[:, piece] = rows.reshape(nodes, lines, LANES)


def send_rows(out_grad, expert_ids, route_weights, nodes, slices, experts, per_group):
    lines = per_group * (out_grad.shape[1] // slices // LANES + 1)
    return pl.pallas_call(
        functools.partial(send_kernel, experts=experts),
        out_shape=[
            jax.ShapeDtypeStruct((nodes, slices, lines, LANES), BF16),
            jax.ShapeDtypeStruct((nodes * per_group, out_grad.shape[0]), F32),
        ],
        compiler_params=pltpu.CompilerParams(vmem_limit_bytes=60 * 1024 * 1024),
        cost_estimate=pl.CostEstimate(flops=40_000_000, bytes_accessed=700_000, transcendentals=0),
    )(out_grad, expert_ids, route_weights)


def pick_kernel(lines_ref, rows_ref, out_ref, slot_weight_ref):
    experts, slots, _ = out_ref.shape
    row_count = rows_ref.shape[0]
    slot = lax.broadcasted_iota(jnp.int32, (slots, row_count), 0).astype(F32)
    for expert in range(experts):
        holds = jnp.where(lines_ref[expert : expert + 1, :] == slot, 1.0, 0.0).astype(BF16)
        out_ref[expert] = jnp.dot(holds, rows_ref[...], preferred_element_type=F32).astype(BF16)
        weights = lines_ref[experts + expert : experts + expert + 1, :].astype(BF16)
        slot_weight_ref[expert] = lax.dot_general(
            jnp.broadcast_to(weights, (8, row_count)),
            holds,
            (((1,), (1,)), ((), ())),
            preferred_element_type=F32,
        )[:1]


def pick(lines, rows, slots):
    experts = lines.shape[0] // 2
    row_count, width = rows.shape
    vmem = pl.BlockSpec(memory_space=pltpu.VMEM)
    return pl.pallas_call(
        pick_kernel,
        in_specs=[vmem, vmem],
        out_specs=[vmem, vmem],
        out_shape=[
            jax.ShapeDtypeStruct((experts, slots, width), BF16),
            jax.ShapeDtypeStruct((experts, 1, slots), F32),
        ],
        compiler_params=pltpu.CompilerParams(vmem_limit_bytes=32 * 1024 * 1024),
        cost_estimate=pl.CostEstimate(
            flops=2 * experts * slots * row_count * width, bytes_accessed=2_500_000, transcendentals=0
        ),
    )(lines, rows)


def as_line(column):
    count = column.shape[0]
    same = lax.broadcasted_iota(jnp.int32, (count, count), 0) == lax.broadcasted_iota(
        jnp.int32, (count, count), 1
    )
    return jnp.sum(jnp.where(same, column, 0.0), axis=0, keepdims=True)


def as_column(line):
    count = line.shape[1]
    same = lax.broadcasted_iota(jnp.int32, (count, count), 0) == lax.broadcasted_iota(
        jnp.int32, (count, count), 1
    )
    return jnp.sum(jnp.where(same, line, 0.0), axis=1, keepdims=True)


def product_kernel(rows_ref, weight_ref, out_ref):
    z_count, slots, width = rows_ref.shape
    rows = rows_ref[...].reshape(z_count * slots, width)
    term = lax.dot_general(
        rows, weight_ref[0], (((1,), (1,)), ((), ())), preferred_element_type=F32
    ).astype(BF16)
    for block in range(out_ref.shape[0]):
        out_ref[block] = term[:, block * LANES : (block + 1) * LANES]


def product(rows, weight):
    z_count, slots, width = rows.shape
    units = weight.shape[1]
    slot_count = z_count * slots
    per_step = 4
    return pl.pallas_call(
        product_kernel,
        grid=(units // LANES // per_step,),
        in_specs=[
            pl.BlockSpec((z_count, slots, width), lambda i: (0, 0, 0)),
            pl.BlockSpec((1, per_step * LANES, width), lambda i: (0, i, 0)),
        ],
        out_specs=pl.BlockSpec((per_step, slot_count, LANES), lambda i: (i, 0, 0)),
        out_shape=jax.ShapeDtypeStruct((units // LANES, slot_count, LANES), BF16),
        compiler_params=pltpu.CompilerParams(vmem_limit_bytes=52 * 1024 * 1024),
        cost_estimate=pl.CostEstimate(
            flops=2 * slot_count * width * units, bytes_accessed=6_000_000, transcendentals=0
        ),
    )(rows, weight)


def dots_kernel(term_ref, hidden_ref, weight_ref, both_ref):
    z_count, _, slots = both_ref.shape
    total = term_ref[0].astype(F32) * hidden_ref[0].astype(F32)
    for block in range(1, term_ref.shape[0]):
        total += term_ref[block].astype(F32) * hidden_ref[block].astype(F32)
    for z in range(z_count):
        both_ref[z, 0:1] = as_line(jnp.sum(total[z * slots : (z + 1) * slots, :], axis=1, keepdims=True))
        both_ref[z, 1:2] = weight_ref[z]


def dots_of(term, hidden, slot_weight):
    blocks, slot_count, lanes = hidden.shape
    z_count, _, slots = slot_weight.shape
    per_step = z_count // 4
    block = pl.BlockSpec((blocks, per_step * slots, lanes), lambda i: (0, i, 0))
    return pl.pallas_call(
        dots_kernel,
        grid=(4,),
        in_specs=[block, block, pl.BlockSpec((per_step, 1, slots), lambda i: (i, 0, 0))],
        out_specs=pl.BlockSpec((per_step, 2, slots), lambda i: (i, 0, 0)),
        out_shape=jax.ShapeDtypeStruct((z_count, 2, slots), F32),
        compiler_params=pltpu.CompilerParams(vmem_limit_bytes=62_390_272),
        cost_estimate=pl.CostEstimate(
            flops=2 * blocks * slot_count * lanes, bytes_accessed=4_000_000, transcendentals=0
        ),
    )(term, hidden, slot_weight)


def gate_kernel(u_ref, gate_ref, up_ref, weight_ref, grad_ref):
    u = u_ref[...].astype(F32)
    a = gate_ref[0].astype(F32)
    b = up_ref[0].astype(F32)
    s = 1.0 / (1.0 + jnp.exp(-a))
    weight = jnp.concatenate([as_column(weight_ref[z, 1:2]) for z in range(weight_ref.shape[0])], axis=0)
    scaled = weight * u
    grad_ref[0, 0] = (scaled * b * s * (1.0 + a * (1.0 - s))).astype(BF16)
    grad_ref[0, 1] = (scaled * a * s).astype(BF16)


def gate(u, gate_pre, up_pre, both):
    z_count, _, slots = both.shape
    slot_count, width = u.shape
    per_step = z_count // 2
    lines = per_step * slots
    return pl.pallas_call(
        gate_kernel,
        grid=(2,),
        in_specs=[
            pl.BlockSpec((lines, width), lambda z: (z, 0)),
            pl.BlockSpec((1, lines, width), lambda z: (0, z, 0)),
            pl.BlockSpec((1, lines, width), lambda z: (0, z, 0)),
            pl.BlockSpec((per_step, 2, slots), lambda z: (z, 0, 0)),
        ],
        out_specs=pl.BlockSpec((1, 2, lines, width), lambda z: (0, 0, z, 0)),
        out_shape=jax.ShapeDtypeStruct((1, 2, slot_count, width), BF16),
        compiler_params=pltpu.CompilerParams(vmem_limit_bytes=62_390_272),
        cost_estimate=pl.CostEstimate(
            flops=30 * slot_count * width, bytes_accessed=2_000_000, transcendentals=slot_count * width
        ),
    )(u, gate_pre, up_pre, both)


def body(out_grad, expert_ids, route_weights, down_weight, gate_pre, up_pre):
    n_node = lax.axis_size("node")
    n_z = lax.axis_size("z")
    n_x = lax.axis_size("x")
    tok_dev, model_width = out_grad.shape
    top_count = expert_ids.shape[1]
    width = model_width // n_x
    cap_group = 4 * tok_dev // n_node
    cap_expert = 2 * tok_dev
    slots = n_x * cap_expert
    row_count = n_node * n_x * cap_group
    tiles = width // LANES

    a = gate_pre[0].astype(F32)
    hidden = (a * (1.0 / (1.0 + jnp.exp(-a))) * up_pre[0].astype(F32)).astype(BF16)
    hidden_all = lax.all_gather(hidden, "x", tiled=True).reshape(n_x, hidden.shape[0], LANES)

    send, chosen = send_rows(out_grad, expert_ids, route_weights, n_node, n_x, n_z, cap_group)
    send = send.reshape(n_node * n_x, cap_group * (tiles + 1), LANES)
    got = lax.all_to_all(send, ("node", "x"), split_axis=0, concat_axis=0, tiled=True)
    got = got.reshape(row_count, tiles + 1, LANES)

    rows = got[:, :tiles].reshape(row_count, width)
    ids = got[:, tiles, :top_count].astype(F32).astype(jnp.int32)
    weights = got[:, tiles, top_count : 2 * top_count].astype(F32)
    my_group = lax.axis_index("node")
    member = (ids - my_group * n_z)[:, None, :] == jnp.arange(n_z, dtype=jnp.int32)[None, :, None]
    named_by = jnp.any(member, axis=2)
    weight_each = jnp.sum(jnp.where(member, weights[:, None, :], 0.0), axis=2)
    row = jnp.arange(row_count, dtype=jnp.int32)
    relay = row // cap_group % n_x
    earlier = (row[None, :] < row[:, None]) & (relay[None, :] == relay[:, None])
    place = jnp.dot(earlier.astype(BF16), named_by.astype(BF16), preferred_element_type=F32)
    slot_each = jnp.where(named_by, (relay * cap_expert).astype(F32)[:, None] + place, -1.0)
    lines = jnp.concatenate([slot_each.T, weight_each.T], axis=0)
    picked, slot_weight = pick(lines, rows, slots)
    taken = lax.all_to_all(picked, "z", split_axis=0, concat_axis=0, tiled=True)

    partial = product(taken, down_weight)
    u = lax.psum_scatter(
        partial.reshape(n_x * n_z * slots, LANES), "x", scatter_dimension=0, tiled=True
    )

    both = dots_of(partial, hidden_all, slot_weight)
    both = lax.all_to_all(both, "z", split_axis=0, concat_axis=0, tiled=True)
    dots = both[:, 0]
    grad_pre = gate(u, gate_pre, up_pre, both)
    slot_iota = jnp.arange(slots, dtype=jnp.int32).astype(F32)
    value = jnp.sum(
        jnp.where(slot_each[:, :, None] == slot_iota, dots[None], 0.0), axis=2
    )
    value = jnp.sum(jnp.where(member, value[:, :, None], 0.0), axis=1)
    value = value.reshape(n_node * n_x, cap_group, top_count)
    back = lax.all_to_all(value, ("node", "x"), split_axis=0, concat_axis=0, tiled=True)
    back = jnp.sum(back.reshape(n_node, n_x, cap_group, top_count), axis=1)
    chosen = chosen.reshape(n_node, cap_group, tok_dev)
    grad_weights = jnp.sum(chosen[..., None] * back[:, :, None, :], axis=(0, 1))
    return (grad_pre, grad_weights)


def solution(mesh):
    devices = mesh.devices
    n_node, n_local = devices.shape
    split = Mesh(devices.reshape(n_node, EPG, n_local // EPG), ("node", "z", "x"))
    first = ("node", "z", "x")
    return jax.shard_map(
        body,
        mesh=split,
        in_specs=(
            P(first, None),
            P(first, None),
            P(first, None),
            P(first, None, None),
            P(first, None, None),
            P(first, None, None),
        ),
        out_specs=(P(first, None, None, None), P(first, None)),
        check_vma=False,
    )
```

```python
import functools

import jax
import jax.numpy as jnp
from jax import lax
from jax.experimental import pallas as pl
from jax.experimental.pallas import tpu as pltpu
from jax.sharding import Mesh
from jax.sharding import PartitionSpec as P

EPG = 8
LANES = 128
F32 = jnp.float32
BF16 = jnp.bfloat16


def iota(shape, axis):
    return lax.broadcasted_iota(jnp.int32, shape, axis)


def one_where(mask):
    return jnp.where(mask, 1.0, 0.0)


def send_kernel(grad_ref, ids_ref, weights_ref, out_ref, chosen_ref, *, experts):
    nodes, slices, lines, _ = out_ref.shape
    tokens, top_count = ids_ref.shape
    tiles = grad_ref.shape[1] // slices // LANES
    parts = tiles + 1
    per_group = lines // parts
    ids = ids_ref[...].astype(F32)
    columns = parts * tokens
    spread = one_where(iota((tokens, columns), 0) == iota((tokens, columns), 1) % tokens)
    named = lax.dot_general(ids, spread, (((0,), (0,)), ((), ())), preferred_element_type=F32)
    named_group = named.astype(jnp.int32) // experts
    shape = (nodes * lines, columns)
    line, column = iota(shape, 0), iota(shape, 1)
    group, rank, part = line // lines, line // parts % per_group, line % parts
    reaches = jnp.zeros(shape, F32)
    for place in range(top_count):
        reaches = jnp.where(named_group[place : place + 1, :] == group, 1.0, reaches)
    square = (columns, columns)
    before = one_where((iota(square, 0) < tokens) & (iota(square, 0) < iota(square, 1) % tokens))
    order = jnp.dot(reaches, before, preferred_element_type=F32)
    chosen = jnp.where(
        (order == rank.astype(F32)) & (part == column // tokens), reaches, 0.0
    ).astype(BF16)
    picks = (chosen_ref.shape[0], nodes * lines)
    first_lines = one_where(iota(picks, 0) * parts == iota(picks, 1)).astype(BF16)
    chosen_ref[...] = jnp.dot(first_lines, chosen, preferred_element_type=F32)[:, :tokens]
    place = (top_count, LANES)
    tail = jnp.dot(ids, one_where(iota(place, 0) == iota(place, 1)), preferred_element_type=F32)
    tail += jnp.dot(
        weights_ref[...].astype(F32),
        one_where(iota(place, 0) + top_count == iota(place, 1)),
        preferred_element_type=F32,
    )
    for piece in range(slices):
        first = piece * tiles
        source = [
            grad_ref[:, (first + tile) * LANES : (first + tile + 1) * LANES].astype(F32) for tile in range(tiles)
        ]
        source = jnp.concatenate(source + [tail], axis=0).astype(BF16)
        rows = jnp.dot(chosen, source, preferred_element_type=F32).astype(BF16)
        out_ref[:, piece] = rows.reshape(nodes, lines, LANES)


def send_rows(out_grad, expert_ids, route_weights, nodes, slices, experts, per_group):
    lines = per_group * (out_grad.shape[1] // slices // LANES + 1)
    return pl.pallas_call(
        functools.partial(send_kernel, experts=experts),
        out_shape=[
            jax.ShapeDtypeStruct((nodes, slices, lines, LANES), BF16),
            jax.ShapeDtypeStruct((nodes * per_group, out_grad.shape[0]), F32),
        ],
        compiler_params=pltpu.CompilerParams(vmem_limit_bytes=60 * 1024 * 1024),
        cost_estimate=pl.CostEstimate(flops=40_000_000, bytes_accessed=700_000, transcendentals=0),
    )(out_grad, expert_ids, route_weights)


def pick_kernel(
    group_ref, tail_ref, rows_ref, out_ref, slot_weight_ref, named_ref, slot_ref, *, relays, per_group, cap_expert
):
    experts, slots, _ = out_ref.shape
    row_count = rows_ref.shape[0]
    top_count = named_ref.shape[0] // 2
    lines = (2 * top_count, LANES)
    named = lax.dot_general(
        one_where(iota(lines, 0) == iota(lines, 1)).astype(BF16),
        tail_ref[...],
        (((1,), (1,)), ((), ())),
        preferred_element_type=F32,
    )
    named_ref[...] = named
    own = named[:top_count] - (group_ref[0] * experts).astype(F32)
    takes, weights = [], []
    for expert in range(experts):
        hits = one_where(own == float(expert))
        takes.append(jnp.sum(hits, axis=0, keepdims=True))
        weights.append(jnp.sum(hits * named[top_count:], axis=0, keepdims=True))
    takes = jnp.concatenate(takes, axis=0)
    square = (row_count, row_count)
    above, here = iota(square, 0), iota(square, 1)
    same_relay = above // per_group % relays == here // per_group % relays
    earlier = one_where((above < here) & same_relay).astype(BF16)
    place = jnp.dot(takes.astype(BF16), earlier, preferred_element_type=F32)
    relay = iota((experts, row_count), 1) // per_group % relays
    slot_each = jnp.where(takes > 0.0, (relay * cap_expert).astype(F32) + place, -1.0)
    slot_ref[...] = slot_each
    slot = iota((slots, row_count), 0).astype(F32)
    for expert in range(experts):
        holds = one_where(slot_each[expert : expert + 1, :] == slot).astype(BF16)
        out_ref[expert] = jnp.dot(holds, rows_ref[...], preferred_element_type=F32).astype(BF16)
        slot_weight_ref[expert] = lax.dot_general(
            jnp.broadcast_to(weights[expert], (8, row_count)).astype(BF16),
            holds,
            (((1,), (1,)), ((), ())),
            preferred_element_type=F32,
        )[:1]


def pick(group, tail, rows, experts, top_count, relays, per_group, cap_expert):
    row_count, width = rows.shape
    slots = relays * cap_expert
    vmem = pl.BlockSpec(memory_space=pltpu.VMEM)
    return pl.pallas_call(
        functools.partial(pick_kernel, relays=relays, per_group=per_group, cap_expert=cap_expert),
        in_specs=[pl.BlockSpec(memory_space=pltpu.SMEM), vmem, vmem],
        out_specs=[vmem] * 4,
        out_shape=[
            jax.ShapeDtypeStruct((experts, slots, width), BF16),
            jax.ShapeDtypeStruct((experts, 1, slots), F32),
            jax.ShapeDtypeStruct((2 * top_count, row_count), F32),
            jax.ShapeDtypeStruct((experts, row_count), F32),
        ],
        compiler_params=pltpu.CompilerParams(vmem_limit_bytes=32 * 1024 * 1024),
        cost_estimate=pl.CostEstimate(
            flops=2 * experts * slots * row_count * width, bytes_accessed=2_500_000, transcendentals=0
        ),
    )(group, tail, rows)


def as_line(column):
    count = column.shape[0]
    same = lax.broadcasted_iota(jnp.int32, (count, count), 0) == lax.broadcasted_iota(
        jnp.int32, (count, count), 1
    )
    return jnp.sum(jnp.where(same, column, 0.0), axis=0, keepdims=True)


def as_column(line):
    count = line.shape[1]
    same = lax.broadcasted_iota(jnp.int32, (count, count), 0) == lax.broadcasted_iota(
        jnp.int32, (count, count), 1
    )
    return jnp.sum(jnp.where(same, line, 0.0), axis=1, keepdims=True)


def product_kernel(rows_ref, weight_ref, out_ref):
    z_count, slots, width = rows_ref.shape
    rows = rows_ref[...].reshape(z_count * slots, width)
    term = lax.dot_general(
        rows, weight_ref[0], (((1,), (1,)), ((), ())), preferred_element_type=F32
    ).astype(BF16)
    for block in range(out_ref.shape[0]):
        out_ref[block] = term[:, block * LANES : (block + 1) * LANES]


def product(rows, weight):
    z_count, slots, width = rows.shape
    units = weight.shape[1]
    slot_count = z_count * slots
    per_step = 4
    return pl.pallas_call(
        product_kernel,
        grid=(units // LANES // per_step,),
        in_specs=[
            pl.BlockSpec((z_count, slots, width), lambda i: (0, 0, 0)),
            pl.BlockSpec((1, per_step * LANES, width), lambda i: (0, i, 0)),
        ],
        out_specs=pl.BlockSpec((per_step, slot_count, LANES), lambda i: (i, 0, 0)),
        out_shape=jax.ShapeDtypeStruct((units // LANES, slot_count, LANES), BF16),
        compiler_params=pltpu.CompilerParams(vmem_limit_bytes=52 * 1024 * 1024),
        cost_estimate=pl.CostEstimate(
            flops=2 * slot_count * width * units, bytes_accessed=6_000_000, transcendentals=0
        ),
    )(rows, weight)


def dots_kernel(term_ref, hidden_ref, weight_ref, both_ref):
    z_count, _, slots = both_ref.shape
    total = term_ref[0].astype(F32) * hidden_ref[0].astype(F32)
    for block in range(1, term_ref.shape[0]):
        total += term_ref[block].astype(F32) * hidden_ref[block].astype(F32)
    for z in range(z_count):
        both_ref[z, 0:1] = as_line(jnp.sum(total[z * slots : (z + 1) * slots, :], axis=1, keepdims=True))
        both_ref[z, 1:2] = weight_ref[z]


def dots_of(term, hidden, slot_weight):
    blocks, slot_count, lanes = hidden.shape
    z_count, _, slots = slot_weight.shape
    per_step = z_count // 4
    block = pl.BlockSpec((blocks, per_step * slots, lanes), lambda i: (0, i, 0))
    return pl.pallas_call(
        dots_kernel,
        grid=(4,),
        in_specs=[block, block, pl.BlockSpec((per_step, 1, slots), lambda i: (i, 0, 0))],
        out_specs=pl.BlockSpec((per_step, 2, slots), lambda i: (i, 0, 0)),
        out_shape=jax.ShapeDtypeStruct((z_count, 2, slots), F32),
        compiler_params=pltpu.CompilerParams(vmem_limit_bytes=52 * 1024 * 1024),
        cost_estimate=pl.CostEstimate(
            flops=2 * blocks * slot_count * lanes, bytes_accessed=4_000_000, transcendentals=0
        ),
    )(term, hidden, slot_weight)


def gate_kernel(u_ref, gate_ref, up_ref, weight_ref, grad_ref):
    u = u_ref[...].astype(F32)
    a = gate_ref[0].astype(F32)
    b = up_ref[0].astype(F32)
    s = 1.0 / (1.0 + jnp.exp(-a))
    weight = jnp.concatenate([as_column(weight_ref[z, 1:2]) for z in range(weight_ref.shape[0])], axis=0)
    scaled = weight * u
    grad_ref[0, 0] = (scaled * b * s * (1.0 + a * (1.0 - s))).astype(BF16)
    grad_ref[0, 1] = (scaled * a * s).astype(BF16)


def gate(u, gate_pre, up_pre, both):
    z_count, _, slots = both.shape
    slot_count, width = u.shape
    per_step = z_count // 2
    lines = per_step * slots
    return pl.pallas_call(
        gate_kernel,
        grid=(2,),
        in_specs=[
            pl.BlockSpec((lines, width), lambda z: (z, 0)),
            pl.BlockSpec((1, lines, width), lambda z: (0, z, 0)),
            pl.BlockSpec((1, lines, width), lambda z: (0, z, 0)),
            pl.BlockSpec((per_step, 2, slots), lambda z: (z, 0, 0)),
        ],
        out_specs=pl.BlockSpec((1, 2, lines, width), lambda z: (0, 0, z, 0)),
        out_shape=jax.ShapeDtypeStruct((1, 2, slot_count, width), BF16),
        compiler_params=pltpu.CompilerParams(vmem_limit_bytes=60 * 1024 * 1024),
        cost_estimate=pl.CostEstimate(
            flops=30 * slot_count * width, bytes_accessed=2_000_000, transcendentals=slot_count * width
        ),
    )(u, gate_pre, up_pre, both)


def body(out_grad, expert_ids, route_weights, down_weight, gate_pre, up_pre):
    n_node = lax.axis_size("node")
    n_z = lax.axis_size("z")
    n_x = lax.axis_size("x")
    tok_dev, model_width = out_grad.shape
    top_count = expert_ids.shape[1]
    width = model_width // n_x
    cap_group = 4 * tok_dev // n_node
    cap_expert = 2 * tok_dev
    slots = n_x * cap_expert
    row_count = n_node * n_x * cap_group
    tiles = width // LANES

    a = gate_pre[0].astype(F32)
    hidden = (a * (1.0 / (1.0 + jnp.exp(-a))) * up_pre[0].astype(F32)).astype(BF16)
    hidden_all = lax.all_gather(hidden, "x", tiled=True).reshape(n_x, hidden.shape[0], LANES)

    send, chosen = send_rows(out_grad, expert_ids, route_weights, n_node, n_x, n_z, cap_group)
    send = send.reshape(n_node * n_x, cap_group * (tiles + 1), LANES)
    got = lax.all_to_all(send, ("node", "x"), split_axis=0, concat_axis=0, tiled=True)
    got = got.reshape(row_count, tiles + 1, LANES)

    rows = got[:, :tiles].reshape(row_count, width)
    group = lax.axis_index("node").astype(jnp.int32).reshape(1)
    picked, slot_weight, named, slot_each = pick(
        group, got[:, tiles], rows, n_z, top_count, n_x, cap_group, cap_expert
    )
    taken = lax.all_to_all(picked, "z", split_axis=0, concat_axis=0, tiled=True)

    partial = product(taken, down_weight)
    u = lax.psum_scatter(
        partial.reshape(n_x * n_z * slots, LANES), "x", scatter_dimension=0, tiled=True
    )

    both = dots_of(partial, hidden_all, slot_weight)
    both = lax.all_to_all(both, "z", split_axis=0, concat_axis=0, tiled=True)
    dots = both[:, 0]
    grad_pre = gate(u, gate_pre, up_pre, both)
    slot_iota = jnp.arange(slots, dtype=jnp.int32).astype(F32)
    value = jnp.sum(
        jnp.where(slot_each.T[:, :, None] == slot_iota, dots[None], 0.0), axis=2
    )
    own = named[:top_count].T - (group[0] * n_z).astype(F32)
    member = own[:, None, :] == jnp.arange(n_z, dtype=jnp.int32).astype(F32)[None, :, None]
    value = jnp.sum(jnp.where(member, value[:, :, None], 0.0), axis=1)
    value = value.reshape(n_node * n_x, cap_group, top_count)
    back = lax.all_to_all(value, ("node", "x"), split_axis=0, concat_axis=0, tiled=True)
    back = jnp.sum(back.reshape(n_node, n_x, cap_group, top_count), axis=1)
    chosen = chosen.reshape(n_node, cap_group, tok_dev)
    grad_weights = jnp.sum(chosen[..., None] * back[:, :, None, :], axis=(0, 1))
    return (grad_pre, grad_weights)


def solution(mesh):
    devices = mesh.devices
    n_node, n_local = devices.shape
    split = Mesh(devices.reshape(n_node, EPG, n_local // EPG), ("node", "z", "x"))
    first = ("node", "z", "x")
    return jax.shard_map(
        body,
        mesh=split,
        in_specs=(
            P(first, None),
            P(first, None),
            P(first, None),
            P(first, None, None),
            P(first, None, None),
            P(first, None, None),
        ),
        out_specs=(P(first, None, None, None), P(first, None)),
        check_vma=False,
    )
```

```python
import functools

import jax
import jax.numpy as jnp
from jax import lax
from jax.experimental import pallas as pl
from jax.experimental.pallas import tpu as pltpu
from jax.sharding import Mesh
from jax.sharding import PartitionSpec as P

EPG = 8
LANES = 128
F32 = jnp.float32
BF16 = jnp.bfloat16


def iota(shape, axis):
    return lax.broadcasted_iota(jnp.int32, shape, axis)


def one_where(mask):
    return jnp.where(mask, 1.0, 0.0)


def send_kernel(grad_ref, ids_ref, weights_ref, out_ref, chosen_ref, *, experts):
    nodes, slices, lines, _ = out_ref.shape
    tokens, top_count = ids_ref.shape
    tiles = grad_ref.shape[1] // slices // LANES
    parts = tiles + 1
    per_group = lines // parts
    ids = ids_ref[...].astype(F32)
    columns = parts * tokens
    spread = one_where(iota((tokens, columns), 0) == iota((tokens, columns), 1) % tokens)
    named = lax.dot_general(ids, spread, (((0,), (0,)), ((), ())), preferred_element_type=F32)
    named_group = named.astype(jnp.int32) // experts
    shape = (nodes * lines, columns)
    line, column = iota(shape, 0), iota(shape, 1)
    group, rank, part = line // lines, line // parts % per_group, line % parts
    reaches = jnp.zeros(shape, F32)
    for place in range(top_count):
        reaches = jnp.where(named_group[place : place + 1, :] == group, 1.0, reaches)
    square = (columns, columns)
    before = one_where((iota(square, 0) < tokens) & (iota(square, 0) < iota(square, 1) % tokens))
    order = jnp.dot(reaches, before, preferred_element_type=F32)
    chosen = jnp.where(
        (order == rank.astype(F32)) & (part == column // tokens), reaches, 0.0
    ).astype(BF16)
    picks = (chosen_ref.shape[0], nodes * lines)
    first_lines = one_where(iota(picks, 0) * parts == iota(picks, 1)).astype(BF16)
    chosen_ref[...] = jnp.dot(first_lines, chosen, preferred_element_type=F32)[:, :tokens]
    place = (top_count, LANES)
    tail = jnp.dot(ids, one_where(iota(place, 0) == iota(place, 1)), preferred_element_type=F32)
    tail += jnp.dot(
        weights_ref[...].astype(F32),
        one_where(iota(place, 0) + top_count == iota(place, 1)),
        preferred_element_type=F32,
    )
    for piece in range(slices):
        first = piece * tiles
        source = [
            grad_ref[:, (first + tile) * LANES : (first + tile + 1) * LANES].astype(F32) for tile in range(tiles)
        ]
        source = jnp.concatenate(source + [tail], axis=0).astype(BF16)
        rows = jnp.dot(chosen, source, preferred_element_type=F32).astype(BF16)
        out_ref[:, piece] = rows.reshape(nodes, lines, LANES)


def send_rows(out_grad, expert_ids, route_weights, nodes, slices, experts, per_group):
    lines = per_group * (out_grad.shape[1] // slices // LANES + 1)
    return pl.pallas_call(
        functools.partial(send_kernel, experts=experts),
        out_shape=[
            jax.ShapeDtypeStruct((nodes, slices, lines, LANES), BF16),
            jax.ShapeDtypeStruct((nodes * per_group, out_grad.shape[0]), F32),
        ],
        compiler_params=pltpu.CompilerParams(vmem_limit_bytes=60 * 1024 * 1024),
        cost_estimate=pl.CostEstimate(flops=40_000_000, bytes_accessed=700_000, transcendentals=0),
    )(out_grad, expert_ids, route_weights)


def pick_kernel(
    group_ref, tail_ref, rows_ref, out_ref, slot_weight_ref, named_ref, slot_ref, *, relays, per_group, cap_expert
):
    experts, slots, _ = out_ref.shape
    row_count = rows_ref.shape[0]
    top_count = named_ref.shape[0] // 2
    lines = (2 * top_count, LANES)
    named = lax.dot_general(
        one_where(iota(lines, 0) == iota(lines, 1)).astype(BF16),
        tail_ref[...],
        (((1,), (1,)), ((), ())),
        preferred_element_type=F32,
    )
    named_ref[...] = named
    own = named[:top_count] - (group_ref[0] * experts).astype(F32)
    takes, weights = [], []
    for expert in range(experts):
        hits = one_where(own == float(expert))
        takes.append(jnp.sum(hits, axis=0, keepdims=True))
        weights.append(jnp.sum(hits * named[top_count:], axis=0, keepdims=True))
    takes = jnp.concatenate(takes, axis=0)
    square = (row_count, row_count)
    above, here = iota(square, 0), iota(square, 1)
    same_relay = above // per_group % relays == here // per_group % relays
    earlier = one_where((above < here) & same_relay).astype(BF16)
    place = jnp.dot(takes.astype(BF16), earlier, preferred_element_type=F32)
    relay = iota((experts, row_count), 1) // per_group % relays
    slot_each = jnp.where(takes > 0.0, (relay * cap_expert).astype(F32) + place, -1.0)
    slot_ref[...] = slot_each
    slot = iota((slots, row_count), 0).astype(F32)
    for expert in range(experts):
        holds = one_where(slot_each[expert : expert + 1, :] == slot).astype(BF16)
        out_ref[expert] = jnp.dot(holds, rows_ref[...], preferred_element_type=F32).astype(BF16)
        slot_weight_ref[expert] = lax.dot_general(
            jnp.broadcast_to(weights[expert], (8, row_count)).astype(BF16),
            holds,
            (((1,), (1,)), ((), ())),
            preferred_element_type=F32,
        )[:1]


def pick(group, tail, rows, experts, top_count, relays, per_group, cap_expert):
    row_count, width = rows.shape
    slots = relays * cap_expert
    vmem = pl.BlockSpec(memory_space=pltpu.VMEM)
    return pl.pallas_call(
        functools.partial(pick_kernel, relays=relays, per_group=per_group, cap_expert=cap_expert),
        in_specs=[pl.BlockSpec(memory_space=pltpu.SMEM), vmem, vmem],
        out_specs=[vmem] * 4,
        out_shape=[
            jax.ShapeDtypeStruct((experts, slots, width), BF16),
            jax.ShapeDtypeStruct((experts, 1, slots), F32),
            jax.ShapeDtypeStruct((2 * top_count, row_count), F32),
            jax.ShapeDtypeStruct((experts, row_count), F32),
        ],
        compiler_params=pltpu.CompilerParams(vmem_limit_bytes=32 * 1024 * 1024),
        cost_estimate=pl.CostEstimate(
            flops=2 * experts * slots * row_count * width, bytes_accessed=2_500_000, transcendentals=0
        ),
    )(group, tail, rows)


def as_line(column):
    count = column.shape[0]
    same = lax.broadcasted_iota(jnp.int32, (count, count), 0) == lax.broadcasted_iota(
        jnp.int32, (count, count), 1
    )
    return jnp.sum(jnp.where(same, column, 0.0), axis=0, keepdims=True)


def as_column(line):
    count = line.shape[1]
    same = lax.broadcasted_iota(jnp.int32, (count, count), 0) == lax.broadcasted_iota(
        jnp.int32, (count, count), 1
    )
    return jnp.sum(jnp.where(same, line, 0.0), axis=1, keepdims=True)


def product_kernel(rows_ref, weight_ref, out_ref):
    z_count, slots, width = rows_ref.shape
    rows = rows_ref[...].reshape(z_count * slots, width)
    term = lax.dot_general(
        rows, weight_ref[0], (((1,), (1,)), ((), ())), preferred_element_type=F32
    ).astype(BF16)
    for block in range(out_ref.shape[0]):
        out_ref[block] = term[:, block * LANES : (block + 1) * LANES]


def product(rows, weight):
    z_count, slots, width = rows.shape
    units = weight.shape[1]
    slot_count = z_count * slots
    per_step = 4
    return pl.pallas_call(
        product_kernel,
        grid=(units // LANES // per_step,),
        in_specs=[
            pl.BlockSpec((z_count, slots, width), lambda i: (0, 0, 0)),
            pl.BlockSpec((1, per_step * LANES, width), lambda i: (0, i, 0)),
        ],
        out_specs=pl.BlockSpec((per_step, slot_count, LANES), lambda i: (i, 0, 0)),
        out_shape=jax.ShapeDtypeStruct((units // LANES, slot_count, LANES), BF16),
        compiler_params=pltpu.CompilerParams(vmem_limit_bytes=52 * 1024 * 1024),
        cost_estimate=pl.CostEstimate(
            flops=2 * slot_count * width * units, bytes_accessed=6_000_000, transcendentals=0
        ),
    )(rows, weight)


def dots_kernel(term_ref, hidden_ref, weight_ref, both_ref):
    z_count, _, slots = both_ref.shape
    total = term_ref[0].astype(F32) * hidden_ref[0].astype(F32)
    for block in range(1, term_ref.shape[0]):
        total += term_ref[block].astype(F32) * hidden_ref[block].astype(F32)
    for z in range(z_count):
        both_ref[z, 0:1] = as_line(jnp.sum(total[z * slots : (z + 1) * slots, :], axis=1, keepdims=True))
        both_ref[z, 1:2] = weight_ref[z]


def dots_of(term, hidden, slot_weight):
    blocks, slot_count, lanes = hidden.shape
    z_count, _, slots = slot_weight.shape
    per_step = z_count // 4
    block = pl.BlockSpec((blocks, per_step * slots, lanes), lambda i: (0, i, 0))
    return pl.pallas_call(
        dots_kernel,
        grid=(4,),
        in_specs=[block, block, pl.BlockSpec((per_step, 1, slots), lambda i: (i, 0, 0))],
        out_specs=pl.BlockSpec((per_step, 2, slots), lambda i: (i, 0, 0)),
        out_shape=jax.ShapeDtypeStruct((z_count, 2, slots), F32),
        compiler_params=pltpu.CompilerParams(vmem_limit_bytes=52 * 1024 * 1024),
        cost_estimate=pl.CostEstimate(
            flops=2 * blocks * slot_count * lanes, bytes_accessed=4_000_000, transcendentals=0
        ),
    )(term, hidden, slot_weight)


def gate_kernel(u_ref, gate_ref, up_ref, weight_ref, grad_ref):
    u = u_ref[...].astype(F32)
    a = gate_ref[0].astype(F32)
    b = up_ref[0].astype(F32)
    s = 1.0 / (1.0 + jnp.exp(-a))
    weight = jnp.concatenate([as_column(weight_ref[z, 1:2]) for z in range(weight_ref.shape[0])], axis=0)
    scaled = weight * u
    grad_ref[0, 0] = (scaled * b * s * (1.0 + a * (1.0 - s))).astype(BF16)
    grad_ref[0, 1] = (scaled * a * s).astype(BF16)


def gate(u, gate_pre, up_pre, both):
    z_count, _, slots = both.shape
    slot_count, width = u.shape
    per_step = z_count // 4
    lines = per_step * slots
    return pl.pallas_call(
        gate_kernel,
        grid=(4,),
        in_specs=[
            pl.BlockSpec((lines, width), lambda z: (z, 0)),
            pl.BlockSpec((1, lines, width), lambda z: (0, z, 0)),
            pl.BlockSpec((1, lines, width), lambda z: (0, z, 0)),
            pl.BlockSpec((per_step, 2, slots), lambda z: (z, 0, 0)),
        ],
        out_specs=pl.BlockSpec((1, 2, lines, width), lambda z: (0, 0, z, 0)),
        out_shape=jax.ShapeDtypeStruct((1, 2, slot_count, width), BF16),
        compiler_params=pltpu.CompilerParams(vmem_limit_bytes=60 * 1024 * 1024),
        cost_estimate=pl.CostEstimate(
            flops=30 * slot_count * width, bytes_accessed=2_000_000, transcendentals=slot_count * width
        ),
    )(u, gate_pre, up_pre, both)


def body(out_grad, expert_ids, route_weights, down_weight, gate_pre, up_pre):
    n_node = lax.axis_size("node")
    n_z = lax.axis_size("z")
    n_x = lax.axis_size("x")
    tok_dev, model_width = out_grad.shape
    top_count = expert_ids.shape[1]
    width = model_width // n_x
    cap_group = 4 * tok_dev // n_node
    cap_expert = 2 * tok_dev
    slots = n_x * cap_expert
    row_count = n_node * n_x * cap_group
    tiles = width // LANES

    a = gate_pre[0].astype(F32)
    hidden = (a * (1.0 / (1.0 + jnp.exp(-a))) * up_pre[0].astype(F32)).astype(BF16)
    hidden_all = lax.all_gather(hidden, "x", tiled=True).reshape(n_x, hidden.shape[0], LANES)

    send, chosen = send_rows(out_grad, expert_ids, route_weights, n_node, n_x, n_z, cap_group)
    send = send.reshape(n_node * n_x, cap_group * (tiles + 1), LANES)
    got = lax.all_to_all(send, ("node", "x"), split_axis=0, concat_axis=0, tiled=True)
    got = got.reshape(row_count, tiles + 1, LANES)

    rows = got[:, :tiles].reshape(row_count, width)
    group = lax.axis_index("node").astype(jnp.int32).reshape(1)
    picked, slot_weight, named, slot_each = pick(
        group, got[:, tiles], rows, n_z, top_count, n_x, cap_group, cap_expert
    )
    taken = lax.all_to_all(picked, "z", split_axis=0, concat_axis=0, tiled=True)

    partial = product(taken, down_weight)
    u = lax.psum_scatter(
        partial.reshape(n_x * n_z * slots, LANES), "x", scatter_dimension=0, tiled=True
    )

    both = dots_of(partial, hidden_all, slot_weight)
    both = lax.all_to_all(both, "z", split_axis=0, concat_axis=0, tiled=True)
    dots = both[:, 0]
    grad_pre = gate(u, gate_pre, up_pre, both)
    slot_iota = jnp.arange(slots, dtype=jnp.int32).astype(F32)
    value = jnp.sum(
        jnp.where(slot_each.T[:, :, None] == slot_iota, dots[None], 0.0), axis=2
    )
    own = named[:top_count].T - (group[0] * n_z).astype(F32)
    member = own[:, None, :] == jnp.arange(n_z, dtype=jnp.int32).astype(F32)[None, :, None]
    value = jnp.sum(jnp.where(member, value[:, :, None], 0.0), axis=1)
    value = value.reshape(n_node * n_x, cap_group, top_count)
    back = lax.all_to_all(value, ("node", "x"), split_axis=0, concat_axis=0, tiled=True)
    back = jnp.sum(back.reshape(n_node, n_x, cap_group, top_count), axis=1)
    chosen = chosen.reshape(n_node, cap_group, tok_dev)
    grad_weights = jnp.sum(chosen[..., None] * back[:, :, None, :], axis=(0, 1))
    return (grad_pre, grad_weights)


def solution(mesh):
    devices = mesh.devices
    n_node, n_local = devices.shape
    split = Mesh(devices.reshape(n_node, EPG, n_local // EPG), ("node", "z", "x"))
    first = ("node", "z", "x")
    return jax.shard_map(
        body,
        mesh=split,
        in_specs=(
            P(first, None),
            P(first, None),
            P(first, None),
            P(first, None, None),
            P(first, None, None),
            P(first, None, None),
        ),
        out_specs=(P(first, None, None, None), P(first, None)),
        check_vma=False,
    )
```
